512 devices in a mesh: seq: 128 (over z, x_lo, y), mp: 4 (over x_hi, core).
Axes of the slice: x: 4 (x_hi: 2, x_lo: 2; x = x_hi * 2 + x_lo), y: 8, z: 8, core: 2. Of those that a mesh axis runs over, the one named last changes fastest.
Arguments:
- hidden_entry_states: bfloat16 [16384, 512], P('seq'), may hold values from -6 to 6
- base_ids: int32 [16384], P('seq'), may hold values from 0 to 4
- mask_index: int32 [2048], P('seq'), may hold values from 0 to 16383, as said below
- first_kernel: bfloat16 [9, 512, 512], P(None, None, 'mp'), may hold values from -0.09375 to 0.09375
- second_kernel: bfloat16 [9, 512, 512], P(None, None, 'mp'), may hold values from -0.09375 to 0.09375
- head_weight: bfloat16 [512, 5], replicated, may hold values from -0.5 to 0.5
Outputs:
- input_grad: bfloat16 [16384, 512], P('seq')
- first_kernel_gradient: float32 [9, 512, 512], P(None, 'seq', 'mp')
- second_kernel_gradient: float32 [9, 512, 512], P(None, 'seq', 'mp')
The draws below stay inside these ranges and needn't reach their ends.
Inputs may be any that keep to these rules, and one draw needn't show every extreme that they name: `mask_index`: each device's 16 entries are distinct positions within its own block of 128 bases, in no particular order.
All inputs are finite; a program needn't handle non-finite values.
Results may differ from the reference program's by a relative error of at most 0.014.
Values may be sent and summed in bfloat16 or wider, within the bound.
A program may use at most 64 MiB of HBM per device.

```python
import jax
import jax.numpy as jnp
from jax import lax

D = 512
K = 9
DILATION_FIRST1 = 2048
DILATION_SECOND2 = 4096
VOCAB = 5
BLK = 128
BASES = 16384
MASK_DEV = 16


def draw_mask_index(key, part):
    block_count = BASES // BLK

    def pick_block(block_index):
        block_key = jax.random.fold_in(key, block_index)
        shuffled = jax.random.permutation(jax.random.fold_in(block_key, 1), BLK).astype(jnp.int32)
        needed = jnp.where(block_index == 0, 0, BLK - 1).astype(jnp.int32)
        special = jnp.logical_or(block_index == 0, block_index == block_count - 1)
        where_needed = jnp.argmax(shuffled == needed).astype(jnp.int32)
        swapped = shuffled.at[where_needed].set(shuffled[0]).at[0].set(needed)
        chosen = jnp.where(special, swapped, shuffled)[:MASK_DEV]
        order = jax.random.permutation(jax.random.fold_in(block_key, 2), MASK_DEV)
        return chosen[order] + block_index * BLK
    picked = jax.vmap(pick_block)(jnp.arange(block_count, dtype=jnp.int32))
    return picked.reshape(-1).astype(jnp.int32)


def set_ends(values, key, low, top_value):
    dims = values.shape
    place = [jax.random.randint(jax.random.fold_in(key, axis), (), 0, dims[axis]) for axis in range(len(dims))]
    values = values.at[tuple(place)].set(low)
    longest = dims.index(max(dims))
    place[longest] = (place[longest] + 1) % dims[longest]
    return values.at[tuple(place)].set(top_value)


def levels(stream_key, extent, shards, low, largest):
    def one(axis_at, parts):
        heights = jax.random.uniform(jax.random.fold_in(jax.random.fold_in(stream_key, 6), axis_at), (parts,), jnp.float32, low / len(shards), largest / len(shards))
        return jnp.repeat(jnp.exp(heights), extent[axis_at] // parts).reshape((-1,) + (1,) * (len(extent) - axis_at - 1))

    factor_of = one(*shards[0])
    for cut in shards[1:]:
        factor_of = factor_of * one(*cut)
    return factor_of


def gaussian(own_key, shape, deviation, limit, split=(), kind=jnp.bfloat16):
    factor_of = levels(own_key, shape, split, -0.22, 0.18) if split else 1.0
    drawn = jax.random.normal(own_key, shape, jnp.float32) * deviation * factor_of
    return jnp.minimum(jnp.maximum(drawn, -limit), limit).astype(kind)


def setup_inputs(seed: int = 0) -> dict:
    seeds = jax.random.split(jax.random.key(seed), 7)
    hidden_entry_states = gaussian(seeds[0], (BASES, D), 1.0, 6.0, ((0, 128),))
    base_ids = set_ends(jax.random.randint(seeds[1], (BASES,), 0, VOCAB), jax.random.fold_in(seeds[1], 1), 0, VOCAB - 1).astype(jnp.int32)
    mask_index = draw_mask_index(jax.random.fold_in(seeds[6], 71), 0)
    first_kernel = gaussian(seeds[3], (K, D, D), (K * D) ** -0.5, 0.09375, ((2, 4),))
    second_kernel = gaussian(seeds[4], (K, D, D), (K * D) ** -0.5, 0.09375, ((2, 4),))
    head_weight = gaussian(seeds[5], (D, VOCAB), (D // 4) ** -0.5, 0.5)
    return dict(hidden_entry_states=hidden_entry_states, base_ids=base_ids, mask_index=mask_index, first_kernel=first_kernel, second_kernel=second_kernel, head_weight=head_weight)


epsilon = 1e-05
root_half = 0.7071067811865476
inv_root_two_pi = 0.3989422804014327

def slide_rows(values, offset):
    row_count = values.shape[0]
    if offset == 0:
        return values
    if abs(offset) >= row_count:
        return jnp.zeros_like(values)
    filler = jnp.zeros((abs(offset),) + values.shape[1:], values.dtype)
    if offset > 0:
        return jnp.concatenate([values[offset:], filler], axis=0)
    return jnp.concatenate([filler, values[:row_count + offset]], axis=0)

def gelu_parts(conv_out):
    normal_cdf = 0.5 * (1.0 + lax.erf(conv_out * root_half))
    gelu_slope = normal_cdf + conv_out * inv_root_two_pi * jnp.exp(-0.5 * conv_out * conv_out)
    return (conv_out * normal_cdf, gelu_slope)

def norm_parts(activation):
    values = activation.astype(jnp.float32)
    centre = lax.optimization_barrier(jnp.mean(values, axis=-1, keepdims=True))
    centred = values - centre
    spread = lax.optimization_barrier(jnp.mean(centred * centred, axis=-1, keepdims=True))
    inverse = lax.rsqrt(spread + epsilon)
    return (centred * inverse, inverse)

def block_forward_pass(source, kernel, dilation):
    tap_count = kernel.shape[0]
    centre_tap = tap_count // 2
    conv_out = jnp.zeros((source.shape[0], kernel.shape[2]), jnp.float32)
    for tap_index in range(tap_count):
        moved = slide_rows(source, dilation * (tap_index - centre_tap))
        conv_out = conv_out + jnp.dot(moved, kernel[tap_index], preferred_element_type=jnp.float32)
    activation, gelu_slope = gelu_parts(conv_out)
    normed, inverse = norm_parts(activation.astype(jnp.bfloat16))
    result = (source.astype(jnp.float32) + normed).astype(jnp.bfloat16)
    return (result, (source, normed, inverse, gelu_slope))

def block_backward_pass(grad_out, saved, kernel, dilation):
    source, normed, inverse, gelu_slope = saved
    tap_count = kernel.shape[0]
    centre_tap = tap_count // 2
    mean_grad = lax.optimization_barrier(jnp.mean(grad_out, axis=-1, keepdims=True))
    mean_cross = lax.optimization_barrier(jnp.mean(grad_out * normed, axis=-1, keepdims=True))
    grad_act = inverse * (grad_out - mean_grad - normed * mean_cross)
    grad_conv = (grad_act * gelu_slope).astype(jnp.bfloat16)
    tap_grads = []
    grad_in = grad_out
    for tap_index in range(tap_count):
        offset = dilation * (tap_index - centre_tap)
        tap_grads.append(jnp.dot(slide_rows(source, offset).T, grad_conv, preferred_element_type=jnp.float32))
        back = jnp.dot(grad_conv, kernel[tap_index].T, preferred_element_type=jnp.float32)
        grad_in = grad_in + slide_rows(back, -offset)
    return (grad_in, jnp.stack(tap_grads, axis=0))

def reference(hidden_entry_states, base_ids, mask_index, first_kernel, second_kernel, head_weight):
    hidden_after_first, first_residuals = block_forward_pass(hidden_entry_states, first_kernel, DILATION_FIRST1)
    hidden_after_second, second_residuals = block_forward_pass(hidden_after_first, second_kernel, DILATION_SECOND2)
    mask_row = jnp.zeros((BASES,), jnp.float32).at[mask_index].set(1.0)
    logits = jnp.dot(hidden_after_second, head_weight, preferred_element_type=jnp.float32)
    exponent = jnp.exp(logits)
    probability = exponent / lax.optimization_barrier(jnp.sum(exponent, axis=1, keepdims=True))
    vocab_cols = lax.broadcasted_iota(jnp.int32, logits.shape, 1)
    onehot = (vocab_cols == base_ids[:, None]).astype(jnp.float32)
    dlogits = mask_row[:, None] * (probability - onehot)
    gradient_after_second = jnp.dot(dlogits, head_weight.astype(jnp.float32).T, precision=lax.Precision.HIGHEST)
    gradient_after_first, second_kernel_gradient = block_backward_pass(gradient_after_second, second_residuals, second_kernel, DILATION_SECOND2)
    gradient_before_first, first_kernel_gradient = block_backward_pass(gradient_after_first, first_residuals, first_kernel, DILATION_FIRST1)
    return (gradient_before_first.astype(jnp.bfloat16), first_kernel_gradient, second_kernel_gradient)
```

```python
import functools
import itertools

import jax
import jax.numpy as jnp
from jax import lax
from jax.experimental import pallas as pl
from jax.experimental.pallas import tpu as pltpu
from jax.sharding import PartitionSpec as P

MESH = pl.DeviceIdType.MESH
ZN, XN, YN, MN = 8, 2, 8, 4
ROWS, CH, OWN, TAPS, VOCAB = 128, 512, 128, 9, 5
RES = ROWS // ZN
MID = TAPS // 2
HOP1, HOP2 = 1, 2
REACH1, REACH2 = 4, 3
HALO1, HALO2 = REACH1 * HOP1, REACH2 * HOP2
PIECE1, PIECE2 = 48, 32
AN, BN = 8, 16
SLICE = CH // AN
MODE = "cube"

epsilon = 1e-05
root_half = 0.7071067811865476
inv_root_two_pi = 0.3989422804014327


def nn(a, b):
    return lax.dot_general(a, b, (((1,), (0,)), ((), ())), preferred_element_type=jnp.float32)


def nt(a, b):
    return lax.dot_general(a, b, (((1,), (1,)), ((), ())), preferred_element_type=jnp.float32)


def split_dot(left, values):
    high = values.astype(jnp.bfloat16)
    low = (values - high.astype(jnp.float32)).astype(jnp.bfloat16)
    return nt(left, high) + nt(left, low)


def gelu_parts(conv_out):
    normal_cdf = 0.5 * (1.0 + lax.erf(conv_out * root_half))
    slope = normal_cdf + conv_out * inv_root_two_pi * jnp.exp(-0.5 * conv_out * conv_out)
    return conv_out * normal_cdf, slope


class Group:
    def __init__(self, coords, mods, place):
        self.coords, self.mods, self.place = coords, mods, place
        every = itertools.product(*(range(n) for n in mods))
        distance = lambda off: sum(min(o, n - o) for o, n in zip(off, mods))
        self.offsets = sorted((o for o in every if any(o)), key=lambda o: -distance(o))

    def moved(self, off, back):
        return tuple(
            c if o == 0 else lax.rem(c + (n - o if back else o), n)
            for c, o, n in zip(self.coords, off, self.mods)
        )

    def index(self, coords):
        at = coords[0]
        for c, n in zip(coords[1:], self.mods[1:]):
            at = at * n + c
        return at

    def me(self):
        return self.index(self.coords)

    def to(self, off):
        coords = self.moved(off, False)
        return self.index(coords), self.place(coords)

    def source(self, off):
        return self.index(self.moved(off, True))


def conv(x_ref, k_ref, hop, reach, acc_ref):
    acc_ref[...] = nn(x_ref[...], k_ref[MID])
    for j in range(-reach, reach + 1):
        if j == 0:
            continue
        n = (ZN - abs(j) * hop) * RES
        to = max(0, -j * hop) * RES
        at = max(0, j * hop) * RES
        acc_ref[to : to + n, :] += nn(x_ref[at : at + n, :], k_ref[MID + j])


def back_conv(d_ref, k_ref, hop, reach, acc_ref):
    acc_ref[...] = nt(d_ref[...], k_ref[MID])
    for j in range(-reach, reach + 1):
        if j == 0:
            continue
        n = (ZN - abs(j) * hop) * RES
        to = max(0, j * hop) * RES
        at = max(0, -j * hop) * RES
        acc_ref[to : to + n, :] += nt(d_ref[at : at + n, :], k_ref[MID + j])


def tap_gradients(ht_ref, d_ref, hop, reach, halo):
    left = ht_ref[...]
    out = []
    for j in range(-reach, reach + 1):
        at = halo - j * hop
        right = d_ref[:, at : at + ZN, :, :].reshape(AN * ROWS, OWN)
        out.append(nn(left, right))
    return out


def pieces(grads, send_ref):
    half = lax.broadcasted_iota(jnp.int32, (8, OWN), 0) < 4
    zero = jnp.zeros((8, OWN), jnp.float32)
    rows = send_ref.shape[1]
    for t in range(SLICE // 8):
        even, odd = [], []
        for p in range(rows // 8):
            a = grads[2 * p][8 * t : 8 * t + 8] if 2 * p < len(grads) else zero
            b = grads[2 * p + 1][8 * t : 8 * t + 8] if 2 * p + 1 < len(grads) else zero
            even.append(jnp.where(half, a, pltpu.roll(b, 4, 0)))
            odd.append(jnp.where(half, pltpu.roll(a, 4, 0), b))
        send_ref[2 * t] = jnp.concatenate(even, axis=0).astype(jnp.bfloat16)
        send_ref[2 * t + 1] = jnp.concatenate(odd, axis=0).astype(jnp.bfloat16)


def kernel(
    h_ref, ids_ref, mask_ref, k1_hbm, k2_hbm, w_ref,
    out_ref, dk1_ref, dk2_ref,
    k1, k2, x0, x1, tsend, tgot, perm, w8, acc, wide,
    act1, slope1, norm1, inv1, slope2, stat,
    hsend0, hsend1, ht0, ht1, d1, d2, dpad1, dpad2,
    psend1, psend2, pgot1, pgot2, rsend, rgot,
    gsend1, gsend2, ggot1, ggot2, zsend, zgot,
    send_sems, recv_sems, local_sems,
):
    f32, bf16 = jnp.float32, jnp.bfloat16
    s, m = lax.axis_index("seq"), lax.axis_index("mp")
    z = s // (XN * YN)
    xl = lax.rem(s // YN, XN)
    y = lax.rem(s, YN)
    seq_of = lambda z, x, y: (z * XN + x) * YN + y

    zs = Group((z,), (ZN,), lambda c: (seq_of(c[0], xl, y), m))
    ms = Group((m,), (MN,), lambda c: (s, c[0]))
    if MODE == "cube":
        z1, y1 = lax.rem(z, 2), lax.rem(y, 2)
        z2, y2 = z // 2, y // 2
        ga = Group((z1, xl, y1), (2, 2, 2), lambda c: (seq_of(z2 * 2 + c[0], c[1], y2 * 2 + c[2]), m))
        gb = Group((z2, y2), (4, 4), lambda c: (seq_of(c[0] * 2 + z1, xl, c[1] * 2 + y1), m))
        seq_at = lambda a, b: seq_of((b // 4) * 2 + a // 4, (a // 2) % 2, (b % 4) * 2 + a % 2)
    else:
        ga = Group((z,), (ZN,), lambda c: (seq_of(c[0], xl, y), m))
        gb = Group((xl, y), (XN, YN), lambda c: (seq_of(z, c[0], c[1]), m))
        seq_at = lambda a, b: a * BN + b

    count = itertools.count()
    started = []

    class Exchange:
        def __init__(self, group):
            self.group = group
            self.ids = {off: next(count) for off in group.offsets}

        def copy(self, off, src, dst, device):
            i = self.ids[off]
            return pltpu.make_async_remote_copy(
                src_ref=src, dst_ref=dst, send_sem=send_sems.at[i], recv_sem=recv_sems.at[i],
                device_id=device, device_id_type=MESH,
            )

        def start(self, src_of, dst_of):
            for off in self.group.offsets:
                to, device = self.group.to(off)
                copy = self.copy(off, src_of(to), dst_of(self.group.me()), device)
                copy.start()
                started.append(copy)

        def wait(self, dst_of):
            for off in self.group.offsets:
                at = dst_of(self.group.source(off))
                self.copy(off, at, at, self.group.to(off)[1]).wait_recv()

    rows16 = lambda i: pl.ds(pl.multiple_of(i * RES, RES), RES)
    lanes = lambda i: pl.ds(pl.multiple_of(i * 128, 128), 128)
    slices = lambda i: pl.ds(pl.multiple_of(i * SLICE, SLICE), SLICE)

    load_h = pltpu.make_async_copy(h_ref.at[rows16(z)], x0.at[rows16(z)], local_sems.at[0])
    load_k1 = pltpu.make_async_copy(k1_hbm, k1, local_sems.at[1])
    load_k2 = pltpu.make_async_copy(k2_hbm, k2, local_sems.at[2])
    load_h.start()
    load_k1.start()
    load_k2.start()

    barrier = pltpu.get_barrier_semaphore()
    seen = 0
    covered = {"cube": (ga, gb), "z": (gb,)}[MODE]
    for group in (zs, ms) + covered:
        for off in group.offsets:
            if MODE == "cube" and group is not zs and group is not ms:
                if not any(off[1:]):
                    continue
            pl.semaphore_signal(barrier, inc=1, device_id=group.to(off)[1], device_id_type=MESH)
            seen += 1

    lane = lax.broadcasted_iota(jnp.int32, (8, 128), 1)
    sub = lax.broadcasted_iota(jnp.int32, (8, 128), 0)
    position = lane + s * ROWS
    hit = position == mask_ref[0]
    for q in range(1, 16):
        hit = jnp.logical_or(hit, position == mask_ref[q])
    target = jnp.where(hit, jnp.broadcast_to(ids_ref[...], (8, 128)), -1).astype(f32)
    target = pltpu.roll(target, z * RES, 1)
    tsend[...] = target
    tgot[z] = target

    p = lax.broadcasted_iota(jnp.int32, (CH, CH), 0)
    a, b, low = p // SLICE, (p // 4) % BN, p % 4
    channel = seq_at(a, b) * 4 + low
    perm[...] = (lax.broadcasted_iota(jnp.int32, (CH, CH), 1) == channel).astype(f32).astype(bf16)

    wt = jnp.transpose(w_ref[...].astype(f32))
    w8[...] = jnp.concatenate([wt, jnp.zeros((8 - VOCAB, CH), f32)], axis=0)
    for dpad, halo in ((dpad1, HALO1), (dpad2, HALO2)):
        zero = jnp.zeros((AN, halo, RES, OWN), bf16)
        dpad[:, 0:halo] = zero
        dpad[:, halo + ZN : 2 * halo + ZN] = zero

    pl.semaphore_wait(barrier, seen)

    move_h = Exchange(zs)
    move_t = Exchange(zs)
    move_h.start(lambda to: h_ref.at[rows16(to)], lambda me: x0.at[rows16(me)])
    move_t.start(lambda to: tsend, lambda me: tgot.at[me])
    load_h.wait()
    load_k1.wait()
    move_h.wait(lambda frm: x0.at[rows16(frm)])

    conv(x0, k1, HOP1, REACH1, acc)
    activation, slope = gelu_parts(acc[...])
    slope1[...] = slope
    act1[m] = activation.astype(bf16)
    gather1 = Exchange(ms)
    gather1.start(lambda to: act1.at[m], lambda me: act1.at[me])

    mine = ga.me()
    hsend0[...] = nt(perm[...], x0[...]).astype(bf16)
    ht0[:, lanes(mine)] = hsend0[slices(mine), :]
    move_t.wait(lambda frm: tgot.at[frm])
    load_k2.wait()
    gather1.wait(lambda frm: act1.at[frm])
    move0 = Exchange(ga)
    move0.start(lambda to: hsend0.at[slices(to)], lambda me: ht0.at[:, lanes(me)])

    values = jnp.concatenate([act1[i] for i in range(MN)], axis=1).astype(f32)
    centred = values - jnp.mean(values, axis=1, keepdims=True)
    inverse = lax.rsqrt(jnp.mean(centred * centred, axis=1, keepdims=True) + epsilon)
    normed = centred * inverse
    for i in range(MN):
        norm1[i] = normed[:, i * 128 : i * 128 + 128]
    inv1[...] = jnp.broadcast_to(inverse, (ROWS, 128))
    x1[...] = (x0[...].astype(f32) + normed).astype(bf16)

    conv(x1, k2, HOP2, REACH2, acc)
    activation, slope = gelu_parts(acc[...])
    slope2[...] = slope
    act2 = activation.astype(bf16)
    values2 = act2.astype(f32)
    w_own = w8[:, lanes(m)]
    sub_own = lax.broadcasted_iota(jnp.int32, (8, OWN), 0)
    left = jnp.where(sub_own == VOCAB, 1.0, w_own).astype(bf16)
    ones = jnp.ones((8, OWN), bf16)
    off_mean = values2 - jnp.mean(values2, axis=1, keepdims=True)
    sums = nt(left, act2)
    squares = split_dot(ones, off_mean * off_mean)
    stat[m] = jnp.where(sub == VOCAB + 1, squares, sums)
    share = Exchange(ms)
    share.start(lambda to: stat.at[m], lambda me: stat.at[me])

    hsend1[...] = nt(perm[...], x1[...]).astype(bf16)
    ht1[:, lanes(mine)] = hsend1[slices(mine), :]
    own_logits = nt(w8[...].astype(bf16), x1[...])
    w_sum = jnp.sum(w8[...], axis=1, keepdims=True)
    turned = pltpu.roll(tgot[:, 0, :], lax.rem(ROWS - z * RES, ROWS), 1)
    targets = jnp.sum(jnp.where(lane // RES == sub, turned, 0.0), axis=0, keepdims=True)
    share.wait(lambda frm: stat.at[frm])

    each = [stat[i] for i in range(MN)]
    total = each[0] + each[1] + each[2] + each[3]
    mean2 = total[VOCAB : VOCAB + 1] * (1.0 / CH)
    spread = total[VOCAB + 1 : VOCAB + 2]
    for part in each:
        apart = part[VOCAB : VOCAB + 1] * (1.0 / OWN) - mean2
        spread = spread + OWN * apart * apart
    inv2 = lax.rsqrt(spread * (1.0 / CH) + epsilon)
    along = inv2 * (total - mean2 * w_sum)
    logits = own_logits + along
    classes = sub < VOCAB
    exponent = jnp.where(classes, jnp.exp(logits), 0.0)
    probability = exponent / jnp.sum(exponent, axis=0, keepdims=True)
    onehot = (sub.astype(f32) == targets).astype(f32)
    dlogits = jnp.where(jnp.logical_and(classes, targets >= 0.0), probability - onehot, 0.0)
    mean_grad = jnp.sum(dlogits * w_sum, axis=0, keepdims=True) * (1.0 / CH)
    mean_cross = jnp.sum(jnp.where(classes, dlogits * along, 0.0), axis=0, keepdims=True) * (1.0 / CH)
    slant = inv2 * mean_cross
    shift = mean_grad - slant * mean2
    packed = jnp.where(sub == 5, inv2, jnp.where(sub == 6, shift, jnp.where(sub == 7, slant, dlogits)))
    by_row = jnp.transpose(jnp.concatenate([packed, jnp.zeros((ROWS - 8, 128), f32)], axis=0))
    grad2 = by_row[:, 0:1] * w_own[0:1]
    for v in range(1, VOCAB):
        grad2 = grad2 + by_row[:, v : v + 1] * w_own[v : v + 1]
    dconv = by_row[:, 5:6] * (grad2 - by_row[:, 6:7] - values2 * by_row[:, 7:8]) * slope2[...]
    dconv = dconv.astype(bf16)
    d2[...] = dconv
    dpad2[mine, HALO2 : HALO2 + ZN] = dconv.reshape(ZN, RES, OWN)

    back_conv(d2, k2, HOP2, REACH2, wide)
    first = grad2
    second = grad2 * norm1[m]
    for i in range(MN):
        part = wide[:, i * 128 : i * 128 + 128].astype(bf16)
        psend2[i] = part
        part = part.astype(f32)
        first = first + part
        second = second + part * norm1[i]
    pgot2[m] = psend2[m]
    reduce2 = Exchange(ms)
    reduce2.start(lambda to: psend2.at[to], lambda me: pgot2.at[me])
    rows_sum = jnp.where(sub == 0, split_dot(ones, first), split_dot(ones, second))
    rsend[...] = rows_sum
    rgot[m] = rows_sum
    reduce_rows = Exchange(ms)
    reduce_rows.start(lambda to: rsend, lambda me: rgot.at[me])

    move1 = Exchange(ga)
    move1.start(lambda to: hsend1.at[slices(to)], lambda me: ht1.at[:, lanes(me)])
    share2 = Exchange(ga)
    share2.start(lambda to: dpad2.at[mine, pl.ds(HALO2, ZN)], lambda me: dpad2.at[me, pl.ds(HALO2, ZN)])

    reduce2.wait(lambda frm: pgot2.at[frm])
    reduce_rows.wait(lambda frm: rgot.at[frm])
    grad1 = grad2
    for i in range(MN):
        grad1 = grad1 + pgot2[i].astype(f32)
    rows_sum = (rgot[0] + rgot[1] + rgot[2] + rgot[3]) * (1.0 / CH)
    by_row = jnp.transpose(jnp.concatenate([rows_sum, jnp.zeros((ROWS - 8, 128), f32)], axis=0))
    dconv = inv1[...] * (grad1 - by_row[:, 0:1] - norm1[m] * by_row[:, 1:2]) * slope1[...]
    dconv = dconv.astype(bf16)
    d1[...] = dconv
    dpad1[mine, HALO1 : HALO1 + ZN] = dconv.reshape(ZN, RES, OWN)
    share1 = Exchange(ga)
    share1.start(lambda to: dpad1.at[mine, pl.ds(HALO1, ZN)], lambda me: dpad1.at[me, pl.ds(HALO1, ZN)])

    back_conv(d1, k1, HOP1, REACH1, wide)
    for i in range(MN):
        psend1[i] = wide[:, i * 128 : i * 128 + 128].astype(bf16)
    pgot1[m] = psend1[m]
    reduce1 = Exchange(ms)
    reduce1.start(lambda to: psend1.at[to], lambda me: pgot1.at[me])

    move1.wait(lambda frm: ht1.at[:, lanes(frm)])
    share2.wait(lambda frm: dpad2.at[frm, pl.ds(HALO2, ZN)])
    owner = gb.me()
    pieces(tap_gradients(ht1, dpad2, HOP2, REACH2, HALO2), gsend2)
    ggot2[owner] = gsend2[owner]
    scatter2 = Exchange(gb)
    scatter2.start(lambda to: gsend2.at[to], lambda me: ggot2.at[me])

    reduce1.wait(lambda frm: pgot1.at[frm])
    for i in range(MN):
        grad1 = grad1 + pgot1[i].astype(f32)
    zsend[...] = grad1.astype(bf16)
    zgot[rows16(z), :] = zsend[rows16(z), :]
    move_back = Exchange(zs)
    move_back.start(lambda to: zsend.at[rows16(to)], lambda me: zgot.at[rows16(me)])

    move0.wait(lambda frm: ht0.at[:, lanes(frm)])
    share1.wait(lambda frm: dpad1.at[frm, pl.ds(HALO1, ZN)])
    pieces(tap_gradients(ht0, dpad1, HOP1, REACH1, HALO1), gsend1)
    ggot1[owner] = gsend1[owner]
    scatter1 = Exchange(gb)
    scatter1.start(lambda to: gsend1.at[to], lambda me: ggot1.at[me])

    move_back.wait(lambda frm: zgot.at[rows16(frm)])
    keep = pltpu.make_async_copy(zgot, out_ref.at[:, lanes(m)], local_sems.at[3])
    keep.start()
    gather_out = Exchange(ms)
    gather_out.start(lambda to: zgot, lambda me: out_ref.at[:, lanes(me)])

    scatter2.wait(lambda frm: ggot2.at[frm])
    grads = ggot2[0].astype(f32)
    for i in range(1, BN):
        grads = grads + ggot2[i].astype(f32)
    dk2_ref[...] = jnp.zeros((TAPS, 4, OWN), f32)
    for j in range(2 * REACH2 + 1):
        dk2_ref[MID - REACH2 + j] = grads[4 * j : 4 * j + 4]

    scatter1.wait(lambda frm: ggot1.at[frm])
    grads = ggot1[0].astype(f32)
    for i in range(1, BN):
        grads = grads + ggot1[i].astype(f32)
    for j in range(TAPS):
        dk1_ref[j] = grads[4 * j : 4 * j + 4]

    gather_out.wait(lambda frm: out_ref.at[:, lanes(frm)])
    keep.wait()
    for copy in started:
        copy.wait_send()


def local(h, ids, mask_index, k1, k2, w):
    f32, bf16 = jnp.float32, jnp.bfloat16
    vmem = pltpu.VMEM
    hbm = pl.BlockSpec(memory_space=pltpu.HBM)
    inside = pl.BlockSpec(memory_space=pltpu.VMEM)
    copies = 8 * 7 + 6 * 3 + 2 * 15 + 8
    return pl.pallas_call(
        kernel,
        out_shape=(
            jax.ShapeDtypeStruct((ROWS, CH), bf16),
            jax.ShapeDtypeStruct((TAPS, 4, OWN), f32),
            jax.ShapeDtypeStruct((TAPS, 4, OWN), f32),
        ),
        in_specs=[hbm, inside, pl.BlockSpec(memory_space=pltpu.SMEM), hbm, hbm, inside],
        out_specs=(hbm, inside, inside),
        scratch_shapes=[
            vmem((TAPS, CH, OWN), bf16),
            vmem((TAPS, CH, OWN), bf16),
            vmem((ROWS, CH), bf16),
            vmem((ROWS, CH), bf16),
            vmem((8, 128), f32),
            vmem((ZN, 8, 128), f32),
            vmem((CH, CH), bf16),
            vmem((8, CH), f32),
            vmem((ROWS, OWN), f32),
            vmem((ROWS, CH), f32),
            vmem((MN, ROWS, OWN), bf16),
            vmem((ROWS, OWN), f32),
            vmem((MN, ROWS, OWN), f32),
            vmem((ROWS, 128), f32),
            vmem((ROWS, OWN), f32),
            vmem((MN, 8, 128), f32),
            vmem((CH, ROWS), bf16),
            vmem((CH, ROWS), bf16),
            vmem((SLICE, AN * ROWS), bf16),
            vmem((SLICE, AN * ROWS), bf16),
            vmem((ROWS, OWN), bf16),
            vmem((ROWS, OWN), bf16),
            vmem((AN, ZN + 2 * HALO1, RES, OWN), bf16),
            vmem((AN, ZN + 2 * HALO2, RES, OWN), bf16),
            vmem((MN, ROWS, OWN), bf16),
            vmem((MN, ROWS, OWN), bf16),
            vmem((MN, ROWS, OWN), bf16),
            vmem((MN, ROWS, OWN), bf16),
            vmem((8, 128), f32),
            vmem((MN, 8, 128), f32),
            vmem((BN, PIECE1, OWN), bf16),
            vmem((BN, PIECE2, OWN), bf16),
            vmem((BN, PIECE1, OWN), bf16),
            vmem((BN, PIECE2, OWN), bf16),
            vmem((ROWS, OWN), bf16),
            vmem((ROWS, OWN), bf16),
            pltpu.SemaphoreType.DMA((copies,)),
            pltpu.SemaphoreType.DMA((copies,)),
            pltpu.SemaphoreType.DMA((4,)),
        ],
        compiler_params=pltpu.CompilerParams(
            collective_id=0, has_side_effects=True, vmem_limit_bytes=40 * 1024 * 1024
        ),
    )(h, ids.reshape(1, ROWS), mask_index, k1, k2, w)


def solution(mesh):
    placed = (P("seq", None), P("seq"), P("seq"), P(None, None, "mp"), P(None, None, "mp"), P())
    return jax.shard_map(
        local,
        mesh=mesh,
        in_specs=placed,
        out_specs=(P("seq", None), P(None, "seq", "mp"), P(None, "seq", "mp")),
        check_vma=False,
    )
```

```python
import functools
import itertools

import jax
import jax.numpy as jnp
from jax import lax
from jax.experimental import pallas as pl
from jax.experimental.pallas import tpu as pltpu
from jax.sharding import PartitionSpec as P

MESH = pl.DeviceIdType.MESH
ZN, XN, YN, MN = 8, 2, 8, 4
ROWS, CH, OWN, TAPS, VOCAB = 128, 512, 128, 9, 5
RES = ROWS // ZN
MID = TAPS // 2
HOP1, HOP2 = 1, 2
REACH1, REACH2 = 4, 3
HALO1, HALO2 = REACH1 * HOP1, REACH2 * HOP2
PIECE1, PIECE2 = 48, 32
AN, BN = 8, 16
SLICE = CH // AN
MODE = "cube"

epsilon = 1e-05
root_half = 0.7071067811865476
inv_root_two_pi = 0.3989422804014327


def nn(a, b):
    return lax.dot_general(a, b, (((1,), (0,)), ((), ())), preferred_element_type=jnp.float32)


def nt(a, b):
    return lax.dot_general(a, b, (((1,), (1,)), ((), ())), preferred_element_type=jnp.float32)


def split_dot(left, values):
    high = values.astype(jnp.bfloat16)
    low = (values - high.astype(jnp.float32)).astype(jnp.bfloat16)
    return nt(left, high) + nt(left, low)


def gelu_parts(conv_out):
    normal_cdf = 0.5 * (1.0 + lax.erf(conv_out * root_half))
    slope = normal_cdf + conv_out * inv_root_two_pi * jnp.exp(-0.5 * conv_out * conv_out)
    return conv_out * normal_cdf, slope


class Group:
    def __init__(self, coords, mods, place):
        self.coords, self.mods, self.place = coords, mods, place
        every = itertools.product(*(range(n) for n in mods))
        distance = lambda off: sum(min(o, n - o) for o, n in zip(off, mods))
        self.offsets = sorted((o for o in every if any(o)), key=lambda o: -distance(o))

    def moved(self, off, back):
        return tuple(
            c if o == 0 else lax.rem(c + (n - o if back else o), n)
            for c, o, n in zip(self.coords, off, self.mods)
        )

    def index(self, coords):
        at = coords[0]
        for c, n in zip(coords[1:], self.mods[1:]):
            at = at * n + c
        return at

    def me(self):
        return self.index(self.coords)

    def to(self, off):
        coords = self.moved(off, False)
        return self.index(coords), self.place(coords)

    def source(self, off):
        return self.index(self.moved(off, True))


def conv(x_ref, k_ref, hop, reach, acc_ref):
    acc_ref[...] = nn(x_ref[...], k_ref[MID])
    for j in range(-reach, reach + 1):
        if j == 0:
            continue
        n = (ZN - abs(j) * hop) * RES
        to = max(0, -j * hop) * RES
        at = max(0, j * hop) * RES
        acc_ref[to : to + n, :] += nn(x_ref[at : at + n, :], k_ref[MID + j])


def back_conv(d_ref, k_ref, hop, reach, acc_ref):
    acc_ref[...] = nt(d_ref[...], k_ref[MID])
    for j in range(-reach, reach + 1):
        if j == 0:
            continue
        n = (ZN - abs(j) * hop) * RES
        to = max(0, j * hop) * RES
        at = max(0, -j * hop) * RES
        acc_ref[to : to + n, :] += nt(d_ref[at : at + n, :], k_ref[MID + j])


def tap_gradients(ht_ref, d_ref, hop, reach, halo):
    left = ht_ref[...]
    out = []
    for j in range(-reach, reach + 1):
        at = halo - j * hop
        right = d_ref[:, at : at + ZN, :, :].reshape(AN * ROWS, OWN)
        out.append(nn(left, right))
    return out


def pieces(grads, send_ref):
    half = lax.broadcasted_iota(jnp.int32, (8, OWN), 0) < 4
    zero = jnp.zeros((8, OWN), jnp.float32)
    rows = send_ref.shape[1]
    for t in range(SLICE // 8):
        even, odd = [], []
        for p in range(rows // 8):
            a = grads[2 * p][8 * t : 8 * t + 8] if 2 * p < len(grads) else zero
            b = grads[2 * p + 1][8 * t : 8 * t + 8] if 2 * p + 1 < len(grads) else zero
            even.append(jnp.where(half, a, pltpu.roll(b, 4, 0)))
            odd.append(jnp.where(half, pltpu.roll(a, 4, 0), b))
        send_ref[2 * t] = jnp.concatenate(even, axis=0).astype(jnp.bfloat16)
        send_ref[2 * t + 1] = jnp.concatenate(odd, axis=0).astype(jnp.bfloat16)


def kernel(
    h_ref, ids_hbm, mask_hbm, k1_hbm, k2_hbm, w_hbm,
    out_ref, dk1_hbm, dk2_hbm,
    ids_ref, mask_ref, w_ref, dk1_ref, dk2_ref, k1, k2, hv, x0, x1, tsend, tgot, perm, w8, acc, wide,
    act1, slope1, norm1, inv1, slope2, stat,
    hsend0, hsend1, ht0, ht1, d1, d2, dpad1, dpad2,
    psend1, psend2, pgot1, pgot2, rsend, rgot,
    gsend1, gsend2, ggot1, ggot2, zsend, zgot,
    send_sems, recv_sems, local_sems,
):
    f32, bf16 = jnp.float32, jnp.bfloat16
    s, m = lax.axis_index("seq"), lax.axis_index("mp")
    z = s // (XN * YN)
    xl = lax.rem(s // YN, XN)
    y = lax.rem(s, YN)
    seq_of = lambda z, x, y: (z * XN + x) * YN + y

    zs = Group((z,), (ZN,), lambda c: (seq_of(c[0], xl, y), m))
    ms = Group((m,), (MN,), lambda c: (s, c[0]))
    if MODE == "cube":
        z1, y1 = lax.rem(z, 2), lax.rem(y, 2)
        z2, y2 = z // 2, y // 2
        ga = Group((z1, xl, y1), (2, 2, 2), lambda c: (seq_of(z2 * 2 + c[0], c[1], y2 * 2 + c[2]), m))
        gb = Group((z2, y2), (4, 4), lambda c: (seq_of(c[0] * 2 + z1, xl, c[1] * 2 + y1), m))
        seq_at = lambda a, b: seq_of((b >> 2) * 2 + (a >> 2), (a >> 1) & 1, (b & 3) * 2 + (a & 1))
    else:
        ga = Group((z,), (ZN,), lambda c: (seq_of(c[0], xl, y), m))
        gb = Group((xl, y), (XN, YN), lambda c: (seq_of(z, c[0], c[1]), m))
        seq_at = lambda a, b: a * BN + b

    count = itertools.count()
    started = []

    class Exchange:
        def __init__(self, group, bytes_of_all):
            self.group, self.i = group, next(count)
            self.all = self.copy(bytes_of_all, bytes_of_all, group.to(group.offsets[0])[1])

        def copy(self, src, dst, device):
            return pltpu.make_async_remote_copy(
                src_ref=src, dst_ref=dst, send_sem=send_sems.at[self.i], recv_sem=recv_sems.at[self.i],
                device_id=device, device_id_type=MESH,
            )

        def start(self, src_of, dst_of):
            for off in self.group.offsets:
                to, device = self.group.to(off)
                self.copy(src_of(to), dst_of(self.group.me()), device).start()
            started.append(self)

        def wait(self):
            self.all.wait_recv()

        def wait_send(self):
            self.all.wait_send()

    rows16 = lambda i: pl.ds(pl.multiple_of(i * RES, RES), RES)
    lanes = lambda i: pl.ds(pl.multiple_of(i * 128, 128), 128)
    slices = lambda i: pl.ds(pl.multiple_of(i * SLICE, SLICE), SLICE)

    barrier = pltpu.get_barrier_semaphore()
    seen = 0
    covered = {"cube": (ga, gb), "z": (gb,)}[MODE]
    for group in (zs, ms) + covered:
        for off in group.offsets:
            if MODE == "cube" and group is not zs and group is not ms:
                if not any(off[1:]):
                    continue
            pl.semaphore_signal(barrier, inc=1, device_id=group.to(off)[1], device_id_type=MESH)
            seen += 1

    load_h = pltpu.make_async_copy(h_ref, hv, local_sems.at[0])
    load_k1 = pltpu.make_async_copy(k1_hbm, k1, local_sems.at[1])
    load_k2 = pltpu.make_async_copy(k2_hbm, k2, local_sems.at[2])
    load_ids = pltpu.make_async_copy(ids_hbm, ids_ref, local_sems.at[4])
    load_mask = pltpu.make_async_copy(mask_hbm, mask_ref, local_sems.at[5])
    load_w = pltpu.make_async_copy(w_hbm, w_ref, local_sems.at[6])
    load_h.start()
    load_k1.start()
    load_ids.start()
    load_mask.start()
    load_w.start()
    load_k2.start()

    load_h.wait()
    pl.semaphore_wait(barrier, seen)

    move_h = Exchange(zs, x0.at[pl.ds(0, ROWS - RES)])
    move_h.start(lambda to: hv.at[rows16(to)], lambda me: x0.at[rows16(me)])
    x0[rows16(z), :] = hv[rows16(z), :]

    load_ids.wait()
    load_mask.wait()
    lane = lax.broadcasted_iota(jnp.int32, (8, 128), 1)
    sub = lax.broadcasted_iota(jnp.int32, (8, 128), 0)
    position = lane + s * ROWS
    hit = position == mask_ref[0]
    for q in range(1, 16):
        hit = jnp.logical_or(hit, position == mask_ref[q])
    target = jnp.where(hit, jnp.broadcast_to(ids_ref[...], (8, 128)), -1).astype(f32)
    target = pltpu.roll(target, z * RES, 1)
    tsend[...] = target
    row = lambda i: pl.ds(i, 1)
    move_t = Exchange(zs, tgot.at[pl.ds(0, ZN - 1)])
    move_t.start(lambda to: tsend.at[row(0)], lambda me: tgot.at[row(me)])
    tgot[row(z), :] = target[0:1]

    p = lax.broadcasted_iota(jnp.int32, (CH, 128), 0)
    a, b, low = p >> 6, (p >> 2) & (BN - 1), p & 3
    channel = seq_at(a, b) * 4 + low - lax.broadcasted_iota(jnp.int32, (CH, 128), 1)
    for i in range(CH // 128):
        perm[:, i * 128 : i * 128 + 128] = (channel == i * 128).astype(f32).astype(bf16)

    load_w.wait()
    w8[...] = jnp.concatenate([w_ref[...].astype(f32), jnp.zeros((8 - VOCAB, CH), f32)], axis=0)
    for dpad, halo in ((dpad1, HALO1), (dpad2, HALO2)):
        zero = jnp.zeros((AN, halo, RES, OWN), bf16)
        dpad[:, 0:halo] = zero
        dpad[:, halo + ZN : 2 * halo + ZN] = zero

    load_k1.wait()
    move_h.wait()

    conv(x0, k1, HOP1, REACH1, acc)
    activation, slope = gelu_parts(acc[...])
    slope1[...] = slope
    act1[m] = activation.astype(bf16)
    gather1 = Exchange(ms, act1.at[pl.ds(0, MN - 1)])
    gather1.start(lambda to: act1.at[m], lambda me: act1.at[me])

    mine = ga.me()
    hsend0[...] = nt(perm[...], x0[...]).astype(bf16)
    ht0[:, lanes(mine)] = hsend0[slices(mine), :]
    move0 = Exchange(ga, ht0.at[:, pl.ds(0, (AN - 1) * ROWS)])
    move0.start(lambda to: hsend0.at[slices(to)], lambda me: ht0.at[:, lanes(me)])
    move_t.wait()
    load_k2.wait()
    gather1.wait()

    values = jnp.concatenate([act1[i] for i in range(MN)], axis=1).astype(f32)
    centred = values - jnp.mean(values, axis=1, keepdims=True)
    inverse = lax.rsqrt(jnp.mean(centred * centred, axis=1, keepdims=True) + epsilon)
    normed = centred * inverse
    for i in range(MN):
        norm1[i] = normed[:, i * 128 : i * 128 + 128]
    inv1[...] = jnp.broadcast_to(inverse, (ROWS, 128))
    x1[...] = (x0[...].astype(f32) + normed).astype(bf16)

    conv(x1, k2, HOP2, REACH2, acc)
    activation, slope = gelu_parts(acc[...])
    slope2[...] = slope
    act2 = activation.astype(bf16)
    values2 = act2.astype(f32)
    w_own = w8[:, lanes(m)]
    sub_own = lax.broadcasted_iota(jnp.int32, (8, OWN), 0)
    left = jnp.where(sub_own == VOCAB, 1.0, w_own).astype(bf16)
    ones = jnp.ones((8, OWN), bf16)
    off_mean = values2 - jnp.mean(values2, axis=1, keepdims=True)
    sums = nt(left, act2)
    squares = split_dot(ones, off_mean * off_mean)
    stat[m] = jnp.where(sub == VOCAB + 1, squares, sums)
    share = Exchange(ms, stat.at[pl.ds(0, MN - 1)])
    share.start(lambda to: stat.at[m], lambda me: stat.at[me])

    hsend1[...] = nt(perm[...], x1[...]).astype(bf16)
    ht1[:, lanes(mine)] = hsend1[slices(mine), :]
    move1 = Exchange(ga, ht1.at[:, pl.ds(0, (AN - 1) * ROWS)])
    move1.start(lambda to: hsend1.at[slices(to)], lambda me: ht1.at[:, lanes(me)])
    own_logits = nt(w8[...].astype(bf16), x1[...])
    w_sum = jnp.sum(w8[...], axis=1, keepdims=True)
    turned = pltpu.roll(tgot[...], lax.rem(ROWS - z * RES, ROWS), 1)
    targets = jnp.sum(jnp.where(lane // RES == sub, turned, 0.0), axis=0, keepdims=True)
    share.wait()

    each = [stat[i] for i in range(MN)]
    total = each[0] + each[1] + each[2] + each[3]
    mean2 = total[VOCAB : VOCAB + 1] * (1.0 / CH)
    spread = total[VOCAB + 1 : VOCAB + 2]
    for part in each:
        apart = part[VOCAB : VOCAB + 1] * (1.0 / OWN) - mean2
        spread = spread + OWN * apart * apart
    inv2 = lax.rsqrt(spread * (1.0 / CH) + epsilon)
    along = inv2 * (total - mean2 * w_sum)
    logits = own_logits + along
    classes = sub < VOCAB
    exponent = jnp.where(classes, jnp.exp(logits), 0.0)
    probability = exponent / jnp.sum(exponent, axis=0, keepdims=True)
    onehot = (sub.astype(f32) == targets).astype(f32)
    dlogits = jnp.where(jnp.logical_and(classes, targets >= 0.0), probability - onehot, 0.0)
    mean_grad = jnp.sum(dlogits * w_sum, axis=0, keepdims=True) * (1.0 / CH)
    mean_cross = jnp.sum(jnp.where(classes, dlogits * along, 0.0), axis=0, keepdims=True) * (1.0 / CH)
    slant = inv2 * mean_cross
    shift = mean_grad - slant * mean2
    packed = jnp.where(sub == 5, inv2, jnp.where(sub == 6, shift, jnp.where(sub == 7, slant, dlogits)))
    by_row = jnp.transpose(jnp.concatenate([packed, jnp.zeros((ROWS - 8, 128), f32)], axis=0))
    grad2 = by_row[:, 0:1] * w_own[0:1]
    for v in range(1, VOCAB):
        grad2 = grad2 + by_row[:, v : v + 1] * w_own[v : v + 1]
    dconv = by_row[:, 5:6] * (grad2 - by_row[:, 6:7] - values2 * by_row[:, 7:8]) * slope2[...]
    dconv = dconv.astype(bf16)
    d2[...] = dconv
    dpad2[mine, HALO2 : HALO2 + ZN] = dconv.reshape(ZN, RES, OWN)

    share2 = Exchange(ga, dpad2.at[pl.ds(0, AN - 1), pl.ds(HALO2, ZN)])
    share2.start(lambda to: dpad2.at[mine, pl.ds(HALO2, ZN)], lambda me: dpad2.at[me, pl.ds(HALO2, ZN)])

    back_conv(d2, k2, HOP2, REACH2, wide)
    first = grad2
    second = grad2 * norm1[m]
    for i in range(MN):
        part = wide[:, i * 128 : i * 128 + 128].astype(bf16)
        psend2[i] = part
        part = part.astype(f32)
        first = first + part
        second = second + part * norm1[i]
    pgot2[m] = psend2[m]
    reduce2 = Exchange(ms, pgot2.at[pl.ds(0, MN - 1)])
    reduce2.start(lambda to: psend2.at[to], lambda me: pgot2.at[me])
    rows_sum = jnp.where(sub == 0, split_dot(ones, first), split_dot(ones, second))
    rsend[...] = rows_sum
    rgot[m] = rows_sum
    reduce_rows = Exchange(ms, rgot.at[pl.ds(0, MN - 1)])
    reduce_rows.start(lambda to: rsend, lambda me: rgot.at[me])

    reduce2.wait()
    reduce_rows.wait()
    grad1 = grad2
    for i in range(MN):
        grad1 = grad1 + pgot2[i].astype(f32)
    rows_sum = (rgot[0] + rgot[1] + rgot[2] + rgot[3]) * (1.0 / CH)
    by_row = jnp.transpose(jnp.concatenate([rows_sum, jnp.zeros((ROWS - 8, 128), f32)], axis=0))
    dconv = inv1[...] * (grad1 - by_row[:, 0:1] - norm1[m] * by_row[:, 1:2]) * slope1[...]
    dconv = dconv.astype(bf16)
    d1[...] = dconv
    dpad1[mine, HALO1 : HALO1 + ZN] = dconv.reshape(ZN, RES, OWN)
    share1 = Exchange(ga, dpad1.at[pl.ds(0, AN - 1), pl.ds(HALO1, ZN)])
    share1.start(lambda to: dpad1.at[mine, pl.ds(HALO1, ZN)], lambda me: dpad1.at[me, pl.ds(HALO1, ZN)])

    back_conv(d1, k1, HOP1, REACH1, wide)
    for i in range(MN):
        psend1[i] = wide[:, i * 128 : i * 128 + 128].astype(bf16)
    pgot1[m] = psend1[m]
    reduce1 = Exchange(ms, pgot1.at[pl.ds(0, MN - 1)])
    reduce1.start(lambda to: psend1.at[to], lambda me: pgot1.at[me])

    move1.wait()
    share2.wait()
    owner = gb.me()
    pieces(tap_gradients(ht1, dpad2, HOP2, REACH2, HALO2), gsend2)
    ggot2[owner] = gsend2[owner]
    scatter2 = Exchange(gb, ggot2.at[pl.ds(0, BN - 1)])
    scatter2.start(lambda to: gsend2.at[to], lambda me: ggot2.at[me])

    reduce1.wait()
    for i in range(MN):
        grad1 = grad1 + pgot1[i].astype(f32)
    zsend[...] = grad1.astype(bf16)
    zgot[rows16(z), :] = zsend[rows16(z), :]
    move_back = Exchange(zs, zgot.at[pl.ds(0, ROWS - RES)])
    move_back.start(lambda to: zsend.at[rows16(to)], lambda me: zgot.at[rows16(me)])

    move0.wait()
    share1.wait()
    pieces(tap_gradients(ht0, dpad1, HOP1, REACH1, HALO1), gsend1)
    ggot1[owner] = gsend1[owner]
    scatter1 = Exchange(gb, ggot1.at[pl.ds(0, BN - 1)])
    scatter1.start(lambda to: gsend1.at[to], lambda me: ggot1.at[me])

    move_back.wait()
    keep = pltpu.make_async_copy(zgot, out_ref.at[:, lanes(m)], local_sems.at[3])
    keep.start()
    gather_out = Exchange(ms, out_ref.at[:, pl.ds(0, CH - OWN)])
    gather_out.start(lambda to: zgot, lambda me: out_ref.at[:, lanes(me)])

    scatter2.wait()
    grads = ggot2[0].astype(f32)
    for i in range(1, BN):
        grads = grads + ggot2[i].astype(f32)
    dk2_ref[...] = jnp.zeros((TAPS, 4, OWN), f32)
    for j in range(2 * REACH2 + 1):
        dk2_ref[MID - REACH2 + j] = grads[4 * j : 4 * j + 4]
    store2 = pltpu.make_async_copy(dk2_ref, dk2_hbm, local_sems.at[7])
    store2.start()

    scatter1.wait()
    grads = ggot1[0].astype(f32)
    for i in range(1, BN):
        grads = grads + ggot1[i].astype(f32)
    for j in range(TAPS):
        dk1_ref[j] = grads[4 * j : 4 * j + 4]
    store1 = pltpu.make_async_copy(dk1_ref, dk1_hbm, local_sems.at[8])
    store1.start()

    gather_out.wait()
    keep.wait()
    store2.wait()
    store1.wait()
    for exchange in started:
        exchange.wait_send()


def local(h, ids, mask_index, k1, k2, w):
    f32, bf16 = jnp.float32, jnp.bfloat16
    vmem = pltpu.VMEM
    hbm = pl.BlockSpec(memory_space=pltpu.HBM)
    copies = 15
    return pl.pallas_call(
        kernel,
        out_shape=(
            jax.ShapeDtypeStruct((ROWS, CH), bf16),
            jax.ShapeDtypeStruct((TAPS, 4, OWN), f32),
            jax.ShapeDtypeStruct((TAPS, 4, OWN), f32),
        ),
        in_specs=[hbm] * 6,
        out_specs=(hbm, hbm, hbm),
        scratch_shapes=[
            vmem((1, ROWS), jnp.int32),
            pltpu.SMEM((16,), jnp.int32),
            vmem((VOCAB, CH), bf16),
            vmem((TAPS, 4, OWN), f32),
            vmem((TAPS, 4, OWN), f32),
            vmem((TAPS, CH, OWN), bf16),
            vmem((TAPS, CH, OWN), bf16),
            vmem((ROWS, CH), bf16),
            vmem((ROWS, CH), bf16),
            vmem((ROWS, CH), bf16),
            vmem((8, 128), f32),
            vmem((ZN, 128), f32),
            vmem((CH, CH), bf16),
            vmem((8, CH), f32),
            vmem((ROWS, OWN), f32),
            vmem((ROWS, CH), f32),
            vmem((MN, ROWS, OWN), bf16),
            vmem((ROWS, OWN), f32),
            vmem((MN, ROWS, OWN), f32),
            vmem((ROWS, 128), f32),
            vmem((ROWS, OWN), f32),
            vmem((MN, 8, 128), f32),
            vmem((CH, ROWS), bf16),
            vmem((CH, ROWS), bf16),
            vmem((SLICE, AN * ROWS), bf16),
            vmem((SLICE, AN * ROWS), bf16),
            vmem((ROWS, OWN), bf16),
            vmem((ROWS, OWN), bf16),
            vmem((AN, ZN + 2 * HALO1, RES, OWN), bf16),
            vmem((AN, ZN + 2 * HALO2, RES, OWN), bf16),
            vmem((MN, ROWS, OWN), bf16),
            vmem((MN, ROWS, OWN), bf16),
            vmem((MN, ROWS, OWN), bf16),
            vmem((MN, ROWS, OWN), bf16),
            vmem((8, 128), f32),
            vmem((MN, 8, 128), f32),
            vmem((BN, PIECE1, OWN), bf16),
            vmem((BN, PIECE2, OWN), bf16),
            vmem((BN, PIECE1, OWN), bf16),
            vmem((BN, PIECE2, OWN), bf16),
            vmem((ROWS, OWN), bf16),
            vmem((ROWS, OWN), bf16),
            pltpu.SemaphoreType.DMA((copies,)),
            pltpu.SemaphoreType.DMA((copies,)),
            pltpu.SemaphoreType.DMA((9,)),
        ],
        compiler_params=pltpu.CompilerParams(
            collective_id=0, has_side_effects=True, vmem_limit_bytes=60 * 1024 * 1024
        ),
    )(h, ids.reshape(1, ROWS), mask_index, k1, k2, w.T)


def solution(mesh):
    placed = (P("seq", None), P("seq"), P("seq"), P(None, None, "mp"), P(None, None, "mp"), P())
    return jax.shard_map(
        local,
        mesh=mesh,
        in_specs=placed,
        out_specs=(P("seq", None), P(None, "seq", "mp"), P(None, "seq", "mp")),
        check_vma=False,
    )
```

```python
import functools
import itertools

import jax
import jax.numpy as jnp
from jax import lax
from jax.experimental import pallas as pl
from jax.experimental.pallas import tpu as pltpu
from jax.sharding import PartitionSpec as P

MESH = pl.DeviceIdType.MESH
ZN, XN, YN, MN = 8, 2, 8, 4
ROWS, CH, OWN, TAPS, VOCAB = 128, 512, 128, 9, 5
RES = ROWS // ZN
MID = TAPS // 2
HOP1, HOP2 = 1, 2
REACH1, REACH2 = 4, 3
HALO1, HALO2 = REACH1 * HOP1, REACH2 * HOP2
PIECE1, PIECE2 = 48, 32
AN, BN = 8, 16
SLICE = CH // AN
MODE = "cube"

epsilon = 1e-05
root_half = 0.7071067811865476
inv_root_two_pi = 0.3989422804014327


def nn(a, b):
    return lax.dot_general(a, b, (((1,), (0,)), ((), ())), preferred_element_type=jnp.float32)


def nt(a, b):
    return lax.dot_general(a, b, (((1,), (1,)), ((), ())), preferred_element_type=jnp.float32)


def split_dot(left, values):
    high = values.astype(jnp.bfloat16)
    low = (values - high.astype(jnp.float32)).astype(jnp.bfloat16)
    return nt(left, high) + nt(left, low)


def gelu_parts(conv_out):
    normal_cdf = 0.5 * (1.0 + lax.erf(conv_out * root_half))
    slope = normal_cdf + conv_out * inv_root_two_pi * jnp.exp(-0.5 * conv_out * conv_out)
    return conv_out * normal_cdf, slope


class Group:
    def __init__(self, coords, mods, place):
        self.coords, self.mods, self.place = coords, mods, place
        every = itertools.product(*(range(n) for n in mods))
        distance = lambda off: sum(min(o, n - o) for o, n in zip(off, mods))
        self.offsets = sorted((o for o in every if any(o)), key=lambda o: -distance(o))

    def moved(self, off, back):
        return tuple(
            c if o == 0 else lax.rem(c + (n - o if back else o), n)
            for c, o, n in zip(self.coords, off, self.mods)
        )

    def index(self, coords):
        at = coords[0]
        for c, n in zip(coords[1:], self.mods[1:]):
            at = at * n + c
        return at

    def me(self):
        return self.index(self.coords)

    def to(self, off):
        coords = self.moved(off, False)
        return self.index(coords), self.place(coords)

    def source(self, off):
        return self.index(self.moved(off, True))


def conv(x_ref, k_ref, hop, reach, acc_ref):
    acc_ref[...] = nn(x_ref[...], k_ref[MID])
    for j in range(-reach, reach + 1):
        if j == 0:
            continue
        n = (ZN - abs(j) * hop) * RES
        to = max(0, -j * hop) * RES
        at = max(0, j * hop) * RES
        acc_ref[to : to + n, :] += nn(x_ref[at : at + n, :], k_ref[MID + j])


def back_conv(d_ref, k_ref, hop, reach, acc_ref):
    acc_ref[...] = nt(d_ref[...], k_ref[MID])
    for j in range(-reach, reach + 1):
        if j == 0:
            continue
        n = (ZN - abs(j) * hop) * RES
        to = max(0, j * hop) * RES
        at = max(0, -j * hop) * RES
        acc_ref[to : to + n, :] += nt(d_ref[at : at + n, :], k_ref[MID + j])


def tap_gradients(ht_ref, d_ref, hop, reach, halo):
    left = ht_ref[...]
    out = []
    for j in range(-reach, reach + 1):
        at = halo - j * hop
        right = d_ref[:, at : at + ZN, :, :].reshape(AN * ROWS, OWN)
        out.append(nn(left, right))
    return out


def pieces(grads, send_ref):
    half = lax.broadcasted_iota(jnp.int32, (8, OWN), 0) < 4
    zero = jnp.zeros((8, OWN), jnp.float32)
    rows = send_ref.shape[1]
    for t in range(SLICE // 8):
        even, odd = [], []
        for p in range(rows // 8):
            a = grads[2 * p][8 * t : 8 * t + 8] if 2 * p < len(grads) else zero
            b = grads[2 * p + 1][8 * t : 8 * t + 8] if 2 * p + 1 < len(grads) else zero
            even.append(jnp.where(half, a, pltpu.roll(b, 4, 0)))
            odd.append(jnp.where(half, pltpu.roll(a, 4, 0), b))
        send_ref[2 * t] = jnp.concatenate(even, axis=0).astype(jnp.bfloat16)
        send_ref[2 * t + 1] = jnp.concatenate(odd, axis=0).astype(jnp.bfloat16)


def kernel(
    h_ref, ids_hbm, mask_hbm, k1_hbm, k2_hbm, w_hbm,
    out_ref, dk1_hbm, dk2_hbm,
    ids_ref, mask_ref, w_ref, dk1_ref, dk2_ref, k1, k2, hv, x0, x1, tsend, tgot, perm, w8, acc, wide,
    act1, slope1, norm1, inv1, slope2, stat,
    hsend0, hsend1, ht0, ht1, d1, d2, dpad1, dpad2,
    psend1, psend2, pgot1, pgot2, rsend, rgot,
    gsend1, gsend2, ggot1, ggot2, zsend, zgot, final,
    send_sems, recv_sems, local_sems, ready_y, ready_x,
):
    f32, bf16 = jnp.float32, jnp.bfloat16
    s, m = lax.axis_index("seq"), lax.axis_index("mp")
    z = s // (XN * YN)
    xl = lax.rem(s // YN, XN)
    y = lax.rem(s, YN)
    seq_of = lambda z, x, y: (z * XN + x) * YN + y

    zs = Group((z,), (ZN,), lambda c: (seq_of(c[0], xl, y), m))
    ms = Group((m,), (MN,), lambda c: (s, c[0]))
    ys = Group((y,), (YN,), lambda c: (seq_of(z, xl, c[0]), m))
    xs = Group((xl,), (XN,), lambda c: (seq_of(z, c[0], y), m))
    core, xh = lax.rem(m, 2), m // 2
    cs = Group((core,), (2,), lambda c: (s, xh * 2 + c[0]))
    zx = Group((z, xh), (ZN, 2), lambda c: (seq_of(c[0], xl, y), c[1] * 2 + core))
    if MODE == "cube":
        z1, y1 = lax.rem(z, 2), lax.rem(y, 2)
        z2, y2 = z // 2, y // 2
        ga = Group((z1, xl, y1), (2, 2, 2), lambda c: (seq_of(z2 * 2 + c[0], c[1], y2 * 2 + c[2]), m))
        gb = Group((z2, y2), (4, 4), lambda c: (seq_of(c[0] * 2 + z1, xl, c[1] * 2 + y1), m))
        seq_at = lambda a, b: seq_of((b >> 2) * 2 + (a >> 2), (a >> 1) & 1, (b & 3) * 2 + (a & 1))
    else:
        ga = Group((z,), (ZN,), lambda c: (seq_of(c[0], xl, y), m))
        gb = Group((xl, y), (XN, YN), lambda c: (seq_of(z, c[0], c[1]), m))
        seq_at = lambda a, b: a * BN + b

    count = itertools.count()
    started = []

    class Exchange:
        def __init__(self, group, bytes_of_all):
            self.group, self.i = group, next(count)
            self.all = self.copy(bytes_of_all, bytes_of_all, group.to(group.offsets[0])[1])

        def copy(self, src, dst, device):
            return pltpu.make_async_remote_copy(
                src_ref=src, dst_ref=dst, send_sem=send_sems.at[self.i], recv_sem=recv_sems.at[self.i],
                device_id=device, device_id_type=MESH,
            )

        def start(self, src_of, dst_of):
            for off in self.group.offsets:
                to, device = self.group.to(off)
                self.copy(src_of(to), dst_of(self.group.me()), device).start()
            if self not in started:
                started.append(self)

        def wait(self):
            self.all.wait_recv()

        def wait_send(self):
            self.all.wait_send()

    rows16 = lambda i: pl.ds(pl.multiple_of(i * RES, RES), RES)
    lanes = lambda i: pl.ds(pl.multiple_of(i * 128, 128), 128)
    slices = lambda i: pl.ds(pl.multiple_of(i * SLICE, SLICE), SLICE)

    barrier = pltpu.get_barrier_semaphore()
    seen = 0
    for group in (zs, ys, ms, xs):
        for off in group.offsets:
            pl.semaphore_signal(barrier, inc=1, device_id=group.to(off)[1], device_id_type=MESH)
            seen += 1

    load_h = pltpu.make_async_copy(h_ref, hv, local_sems.at[0])
    load_k1 = pltpu.make_async_copy(k1_hbm, k1, local_sems.at[1])
    load_k2 = pltpu.make_async_copy(k2_hbm, k2, local_sems.at[2])
    load_ids = pltpu.make_async_copy(ids_hbm, ids_ref, local_sems.at[4])
    load_mask = pltpu.make_async_copy(mask_hbm, mask_ref, local_sems.at[5])
    load_w = pltpu.make_async_copy(w_hbm, w_ref, local_sems.at[6])
    load_h.start()
    load_k1.start()
    load_ids.start()
    load_mask.start()
    load_w.start()
    load_k2.start()

    load_h.wait()
    pl.semaphore_wait(barrier, seen)

    move_h = Exchange(zs, x0.at[pl.ds(0, ROWS - RES)])
    move_h.start(lambda to: hv.at[rows16(to)], lambda me: x0.at[rows16(me)])
    x0[rows16(z), :] = hv[rows16(z), :]
    for off in ys.offsets:
        pl.semaphore_signal(ready_y, inc=1, device_id=ys.to(off)[1], device_id_type=MESH)

    load_ids.wait()
    load_mask.wait()
    lane = lax.broadcasted_iota(jnp.int32, (8, 128), 1)
    sub = lax.broadcasted_iota(jnp.int32, (8, 128), 0)
    position = lane + s * ROWS
    hit = position == mask_ref[0]
    for q in range(1, 16):
        hit = jnp.logical_or(hit, position == mask_ref[q])
    target = jnp.where(hit, jnp.broadcast_to(ids_ref[...], (8, 128)), -1).astype(f32)
    target = pltpu.roll(target, z * RES, 1)
    tsend[...] = target
    row = lambda i: pl.ds(i, 1)
    move_t = Exchange(zs, tgot.at[pl.ds(0, ZN - 1)])
    move_t.start(lambda to: tsend.at[row(0)], lambda me: tgot.at[row(me)])
    tgot[row(z), :] = target[0:1]

    p = lax.broadcasted_iota(jnp.int32, (CH, 128), 0)
    a, b, low = p >> 6, (p >> 2) & (BN - 1), p & 3
    channel = seq_at(a, b) * 4 + low - lax.broadcasted_iota(jnp.int32, (CH, 128), 1)
    for i in range(CH // 128):
        perm[:, i * 128 : i * 128 + 128] = (channel == i * 128).astype(f32).astype(bf16)

    load_w.wait()
    w8[...] = jnp.concatenate([w_ref[...].astype(f32), jnp.zeros((8 - VOCAB, CH), f32)], axis=0)
    for dpad, halo in ((dpad1, HALO1), (dpad2, HALO2)):
        zero = jnp.zeros((AN, halo, RES, OWN), bf16)
        dpad[:, 0:halo] = zero
        dpad[:, halo + ZN : 2 * halo + ZN] = zero

    load_k1.wait()
    move_h.wait()

    conv(x0, k1, HOP1, REACH1, acc)
    activation, slope = gelu_parts(acc[...])
    slope1[...] = slope
    act1[m] = activation.astype(bf16)
    gather1 = Exchange(ms, act1.at[pl.ds(0, MN - 1)])
    gather1.start(lambda to: act1.at[m], lambda me: act1.at[me])

    pl.semaphore_wait(ready_y, YN - 1)
    pl.semaphore_signal(ready_x, inc=1, device_id=xs.to((1,))[1], device_id_type=MESH)

    mine = ga.me()
    hsend0[...] = nt(perm[...], x0[...]).astype(bf16)
    ht0[:, lanes(mine)] = hsend0[slices(mine), :]
    pl.semaphore_wait(ready_x, XN - 1)
    move0 = Exchange(ga, ht0.at[:, pl.ds(0, (AN - 1) * ROWS)])
    move0.start(lambda to: hsend0.at[slices(to)], lambda me: ht0.at[:, lanes(me)])
    move_t.wait()
    load_k2.wait()
    gather1.wait()

    values = jnp.concatenate([act1[i] for i in range(MN)], axis=1).astype(f32)
    centred = values - jnp.mean(values, axis=1, keepdims=True)
    inverse = lax.rsqrt(jnp.mean(centred * centred, axis=1, keepdims=True) + epsilon)
    normed = centred * inverse
    for i in range(MN):
        norm1[i] = normed[:, i * 128 : i * 128 + 128]
    inv1[...] = jnp.broadcast_to(inverse, (ROWS, 128))
    x1[...] = (x0[...].astype(f32) + normed).astype(bf16)

    conv(x1, k2, HOP2, REACH2, acc)
    activation, slope = gelu_parts(acc[...])
    slope2[...] = slope
    act2 = activation.astype(bf16)
    values2 = act2.astype(f32)
    w_own = w8[:, lanes(m)]
    sub_own = lax.broadcasted_iota(jnp.int32, (8, OWN), 0)
    left = jnp.where(sub_own == VOCAB, 1.0, w_own).astype(bf16)
    ones = jnp.ones((8, OWN), bf16)
    off_mean = values2 - jnp.mean(values2, axis=1, keepdims=True)
    sums = nt(left, act2)
    squares = split_dot(ones, off_mean * off_mean)
    stat[m] = jnp.where(sub == VOCAB + 1, squares, sums)
    share = Exchange(ms, stat.at[pl.ds(0, MN - 1)])
    share.start(lambda to: stat.at[m], lambda me: stat.at[me])

    hsend1[...] = nt(perm[...], x1[...]).astype(bf16)
    ht1[:, lanes(mine)] = hsend1[slices(mine), :]
    move1 = Exchange(ga, ht1.at[:, pl.ds(0, (AN - 1) * ROWS)])
    move1.start(lambda to: hsend1.at[slices(to)], lambda me: ht1.at[:, lanes(me)])
    own_logits = nt(w8[...].astype(bf16), x1[...])
    w_sum = jnp.sum(w8[...], axis=1, keepdims=True)
    turned = pltpu.roll(tgot[...], lax.rem(ROWS - z * RES, ROWS), 1)
    targets = jnp.sum(jnp.where(lane // RES == sub, turned, 0.0), axis=0, keepdims=True)
    share.wait()

    each = [stat[i] for i in range(MN)]
    total = each[0] + each[1] + each[2] + each[3]
    mean2 = total[VOCAB : VOCAB + 1] * (1.0 / CH)
    spread = total[VOCAB + 1 : VOCAB + 2]
    for part in each:
        apart = part[VOCAB : VOCAB + 1] * (1.0 / OWN) - mean2
        spread = spread + OWN * apart * apart
    inv2 = lax.rsqrt(spread * (1.0 / CH) + epsilon)
    along = inv2 * (total - mean2 * w_sum)
    logits = own_logits + along
    classes = sub < VOCAB
    exponent = jnp.where(classes, jnp.exp(logits), 0.0)
    probability = exponent / jnp.sum(exponent, axis=0, keepdims=True)
    onehot = (sub.astype(f32) == targets).astype(f32)
    dlogits = jnp.where(jnp.logical_and(classes, targets >= 0.0), probability - onehot, 0.0)
    mean_grad = jnp.sum(dlogits * w_sum, axis=0, keepdims=True) * (1.0 / CH)
    mean_cross = jnp.sum(jnp.where(classes, dlogits * along, 0.0), axis=0, keepdims=True) * (1.0 / CH)
    slant = inv2 * mean_cross
    shift = mean_grad - slant * mean2
    packed = jnp.where(sub == 5, inv2, jnp.where(sub == 6, shift, jnp.where(sub == 7, slant, dlogits)))
    by_row = jnp.transpose(jnp.concatenate([packed, jnp.zeros((ROWS - 8, 128), f32)], axis=0))
    grad2 = by_row[:, 0:1] * w_own[0:1]
    for v in range(1, VOCAB):
        grad2 = grad2 + by_row[:, v : v + 1] * w_own[v : v + 1]
    dconv = by_row[:, 5:6] * (grad2 - by_row[:, 6:7] - values2 * by_row[:, 7:8]) * slope2[...]
    dconv = dconv.astype(bf16)
    d2[...] = dconv
    dpad2[mine, HALO2 : HALO2 + ZN] = dconv.reshape(ZN, RES, OWN)

    back_conv(d2, k2, HOP2, REACH2, wide)
    first = grad2
    second = grad2 * norm1[m]
    for i in range(MN):
        part = wide[:, i * 128 : i * 128 + 128].astype(bf16)
        psend2[i] = part
        part = part.astype(f32)
        first = first + part
        second = second + part * norm1[i]
    pgot2[m] = psend2[m]
    reduce2 = Exchange(ms, pgot2.at[pl.ds(0, MN - 1)])
    reduce2.start(lambda to: psend2.at[to], lambda me: pgot2.at[me])
    rows_sum = jnp.where(sub == 0, split_dot(ones, first), split_dot(ones, second))
    rsend[...] = rows_sum
    rgot[m] = rows_sum
    reduce_rows = Exchange(ms, rgot.at[pl.ds(0, MN - 1)])
    reduce_rows.start(lambda to: rsend, lambda me: rgot.at[me])

    share2 = Exchange(ga, dpad2.at[pl.ds(0, AN - 1), pl.ds(HALO2, ZN)])
    share2.start(lambda to: dpad2.at[mine, pl.ds(HALO2, ZN)], lambda me: dpad2.at[me, pl.ds(HALO2, ZN)])
    reduce2.wait()
    reduce_rows.wait()
    grad1 = grad2
    for i in range(MN):
        grad1 = grad1 + pgot2[i].astype(f32)
    rows_sum = (rgot[0] + rgot[1] + rgot[2] + rgot[3]) * (1.0 / CH)
    by_row = jnp.transpose(jnp.concatenate([rows_sum, jnp.zeros((ROWS - 8, 128), f32)], axis=0))
    dconv = inv1[...] * (grad1 - by_row[:, 0:1] - norm1[m] * by_row[:, 1:2]) * slope1[...]
    dconv = dconv.astype(bf16)
    d1[...] = dconv
    dpad1[mine, HALO1 : HALO1 + ZN] = dconv.reshape(ZN, RES, OWN)
    share1 = Exchange(ga, dpad1.at[pl.ds(0, AN - 1), pl.ds(HALO1, ZN)])
    share1.start(lambda to: dpad1.at[mine, pl.ds(HALO1, ZN)], lambda me: dpad1.at[me, pl.ds(HALO1, ZN)])

    back_conv(d1, k1, HOP1, REACH1, wide)
    for c in range(2):
        for i in range(2):
            at = (i * 2 + c) * 128
            psend1[c, i] = wide[:, at : at + 128].astype(bf16)
    reduce1 = Exchange(cs, pgot1)
    reduce1.start(lambda to: psend1.at[to], lambda me: pgot1)
    wide[:, lanes(m)] += grad1

    move1.wait()
    share2.wait()
    owner = gb.me()
    pieces(tap_gradients(ht1, dpad2, HOP2, REACH2, HALO2), gsend2)
    ggot2[owner] = gsend2[owner]
    scatter2 = Exchange(gb, ggot2.at[pl.ds(0, BN - 1)])
    scatter2.start(lambda to: gsend2.at[to], lambda me: ggot2.at[me])

    reduce1.wait()
    for i in range(2):
        zsend[i] = (wide[:, lanes(i * 2 + core)] + pgot1[i].astype(f32)).astype(bf16)
    zgot[zx.me()] = zsend[:, rows16(z), :]
    move_back = Exchange(zx, zgot.at[pl.ds(0, 2 * ZN - 1)])
    move_back.start(lambda to: zsend.at[:, rows16(to // 2)], lambda me: zgot.at[me])

    move0.wait()
    share1.wait()
    pieces(tap_gradients(ht0, dpad1, HOP1, REACH1, HALO1), gsend1)
    ggot1[owner] = gsend1[owner]
    scatter1 = Exchange(gb, ggot1.at[pl.ds(0, BN - 1)])
    scatter1.start(lambda to: gsend1.at[to], lambda me: ggot1.at[me])

    move_back.wait()
    gather_out = Exchange(cs, out_ref.at[:, pl.ds(0, 2 * OWN)])
    keep = []
    for i in range(2):
        for r in range(ZN):
            total = zgot[2 * r, i].astype(f32) + zgot[2 * r + 1, i].astype(f32)
            final[i, r * RES : r * RES + RES] = total.astype(bf16)
        place = out_ref.at[:, lanes(i * 2 + core)]
        keep.append(pltpu.make_async_copy(final.at[i], place, local_sems.at[3 + 6 * i]))
        keep[i].start()
        gather_out.start(lambda to: final.at[i], lambda me: place)

    scatter2.wait()
    grads = ggot2[0].astype(f32)
    for i in range(1, BN):
        grads = grads + ggot2[i].astype(f32)
    dk2_ref[...] = jnp.zeros((TAPS, 4, OWN), f32)
    for j in range(2 * REACH2 + 1):
        dk2_ref[MID - REACH2 + j] = grads[4 * j : 4 * j + 4]
    store2 = pltpu.make_async_copy(dk2_ref, dk2_hbm, local_sems.at[7])
    store2.start()

    scatter1.wait()
    grads = ggot1[0].astype(f32)
    for i in range(1, BN):
        grads = grads + ggot1[i].astype(f32)
    for j in range(TAPS):
        dk1_ref[j] = grads[4 * j : 4 * j + 4]
    store1 = pltpu.make_async_copy(dk1_ref, dk1_hbm, local_sems.at[8])
    store1.start()

    gather_out.wait()
    for copy in keep:
        copy.wait()
    store2.wait()
    store1.wait()
    for exchange in started:
        exchange.wait_send()


def local(h, ids, mask_index, k1, k2, w):
    f32, bf16 = jnp.float32, jnp.bfloat16
    vmem = pltpu.VMEM
    hbm = pl.BlockSpec(memory_space=pltpu.HBM)
    copies = 15
    return pl.pallas_call(
        kernel,
        out_shape=(
            jax.ShapeDtypeStruct((ROWS, CH), bf16),
            jax.ShapeDtypeStruct((TAPS, 4, OWN), f32),
            jax.ShapeDtypeStruct((TAPS, 4, OWN), f32),
        ),
        in_specs=[hbm] * 6,
        out_specs=(hbm, hbm, hbm),
        scratch_shapes=[
            vmem((1, ROWS), jnp.int32),
            pltpu.SMEM((16,), jnp.int32),
            vmem((VOCAB, CH), bf16),
            vmem((TAPS, 4, OWN), f32),
            vmem((TAPS, 4, OWN), f32),
            vmem((TAPS, CH, OWN), bf16),
            vmem((TAPS, CH, OWN), bf16),
            vmem((ROWS, CH), bf16),
            vmem((ROWS, CH), bf16),
            vmem((ROWS, CH), bf16),
            vmem((8, 128), f32),
            vmem((ZN, 128), f32),
            vmem((CH, CH), bf16),
            vmem((8, CH), f32),
            vmem((ROWS, OWN), f32),
            vmem((ROWS, CH), f32),
            vmem((MN, ROWS, OWN), bf16),
            vmem((ROWS, OWN), f32),
            vmem((MN, ROWS, OWN), f32),
            vmem((ROWS, 128), f32),
            vmem((ROWS, OWN), f32),
            vmem((MN, 8, 128), f32),
            vmem((CH, ROWS), bf16),
            vmem((CH, ROWS), bf16),
            vmem((SLICE, AN * ROWS), bf16),
            vmem((SLICE, AN * ROWS), bf16),
            vmem((ROWS, OWN), bf16),
            vmem((ROWS, OWN), bf16),
            vmem((AN, ZN + 2 * HALO1, RES, OWN), bf16),
            vmem((AN, ZN + 2 * HALO2, RES, OWN), bf16),
            vmem((2, 2, ROWS, OWN), bf16),
            vmem((MN, ROWS, OWN), bf16),
            vmem((2, ROWS, OWN), bf16),
            vmem((MN, ROWS, OWN), bf16),
            vmem((8, 128), f32),
            vmem((MN, 8, 128), f32),
            vmem((BN, PIECE1, OWN), bf16),
            vmem((BN, PIECE2, OWN), bf16),
            vmem((BN, PIECE1, OWN), bf16),
            vmem((BN, PIECE2, OWN), bf16),
            vmem((2, ROWS, OWN), bf16),
            vmem((2 * ZN, 2, RES, OWN), bf16),
            vmem((2, ROWS, OWN), bf16),
            pltpu.SemaphoreType.DMA((copies,)),
            pltpu.SemaphoreType.DMA((copies,)),
            pltpu.SemaphoreType.DMA((10,)),
            pltpu.SemaphoreType.REGULAR,
            pltpu.SemaphoreType.REGULAR,
        ],
        compiler_params=pltpu.CompilerParams(
            collective_id=0, has_side_effects=True, vmem_limit_bytes=60 * 1024 * 1024
        ),
    )(h, ids.reshape(1, ROWS), mask_index, k1, k2, w.T)


def solution(mesh):
    placed = (P("seq", None), P("seq"), P("seq"), P(None, None, "mp"), P(None, None, "mp"), P())
    return jax.shard_map(
        local,
        mesh=mesh,
        in_specs=placed,
        out_specs=(P("seq", None), P(None, "seq", "mp"), P(None, "seq", "mp")),
        check_vma=False,
    )
```

```python
import functools
import itertools

import jax
import jax.numpy as jnp
from jax import lax
from jax.experimental import pallas as pl
from jax.experimental.pallas import tpu as pltpu
from jax.sharding import PartitionSpec as P

MESH = pl.DeviceIdType.MESH
ZN, XN, YN, MN = 8, 2, 8, 4
ROWS, CH, OWN, TAPS, VOCAB = 128, 512, 128, 9, 5
RES = ROWS // ZN
MID = TAPS // 2
HOP1, HOP2 = 1, 2
REACH1, REACH2 = 4, 3
HALO1, HALO2 = REACH1 * HOP1, REACH2 * HOP2
PIECE = 64
AN, BN = 8, 16
SLICE = CH // AN
MODE = "cube"

epsilon = 1e-05
root_half = 0.7071067811865476
inv_root_two_pi = 0.3989422804014327


def nn(a, b):
    return lax.dot_general(a, b, (((1,), (0,)), ((), ())), preferred_element_type=jnp.float32)


def nt(a, b):
    return lax.dot_general(a, b, (((1,), (1,)), ((), ())), preferred_element_type=jnp.float32)


def split_dot(left, values):
    high = values.astype(jnp.bfloat16)
    low = (values - high.astype(jnp.float32)).astype(jnp.bfloat16)
    return nt(left, high) + nt(left, low)


def gelu_parts(conv_out):
    normal_cdf = 0.5 * (1.0 + lax.erf(conv_out * root_half))
    slope = normal_cdf + conv_out * inv_root_two_pi * jnp.exp(-0.5 * conv_out * conv_out)
    return conv_out * normal_cdf, slope


class Group:
    def __init__(self, coords, mods, place):
        self.coords, self.mods, self.place = coords, mods, place
        every = itertools.product(*(range(n) for n in mods))
        distance = lambda off: sum(min(o, n - o) for o, n in zip(off, mods))
        self.offsets = sorted((o for o in every if any(o)), key=lambda o: -distance(o))

    def moved(self, off, back):
        return tuple(
            c if o == 0 else lax.rem(c + (n - o if back else o), n)
            for c, o, n in zip(self.coords, off, self.mods)
        )

    def index(self, coords):
        at = coords[0]
        for c, n in zip(coords[1:], self.mods[1:]):
            at = at * n + c
        return at

    def me(self):
        return self.index(self.coords)

    def to(self, off):
        coords = self.moved(off, False)
        return self.index(coords), self.place(coords)

    def source(self, off):
        return self.index(self.moved(off, True))


def conv(x_ref, k_ref, hop, reach, acc_ref):
    acc_ref[...] = nn(x_ref[...], k_ref[MID])
    for j in range(-reach, reach + 1):
        if j == 0:
            continue
        n = (ZN - abs(j) * hop) * RES
        to = max(0, -j * hop) * RES
        at = max(0, j * hop) * RES
        acc_ref[to : to + n, :] += nn(x_ref[at : at + n, :], k_ref[MID + j])


def back_conv(d_ref, k_ref, hop, reach, acc_ref):
    acc_ref[...] = nt(d_ref[...], k_ref[MID])
    for j in range(-reach, reach + 1):
        if j == 0:
            continue
        n = (ZN - abs(j) * hop) * RES
        to = max(0, j * hop) * RES
        at = max(0, -j * hop) * RES
        acc_ref[to : to + n, :] += nt(d_ref[at : at + n, :], k_ref[MID + j])


def back_conv_part(d_ref, k_ref, hop, reach, part, acc_ref):
    channels = pl.ds(pl.multiple_of(part * OWN, OWN), OWN)
    acc_ref[...] = nt(d_ref[...], k_ref[MID, channels, :])
    for j in range(-reach, reach + 1):
        if j == 0:
            continue
        n = (ZN - abs(j) * hop) * RES
        to = max(0, j * hop) * RES
        at = max(0, -j * hop) * RES
        acc_ref[to : to + n, :] += nt(d_ref[at : at + n, :], k_ref[MID + j, channels, :])


def tap_gradients(ht_ref, d_ref, hop, reach, halo):
    left = ht_ref[...]
    out = []
    for j in range(-reach, reach + 1):
        at = halo - j * hop
        right = d_ref[:, at : at + ZN, :, :].reshape(AN * ROWS, OWN)
        out.append(nn(left, right))
    return out


def pieces(grads, send_ref, first):
    half = lax.broadcasted_iota(jnp.int32, (8, OWN), 0) < 4
    for t in range(SLICE // 8):
        even, odd = [], []
        for a, b in zip(grads[::2], grads[1::2]):
            a, b = a[8 * t : 8 * t + 8], b[8 * t : 8 * t + 8]
            even.append(jnp.where(half, a, pltpu.roll(b, 4, 0)))
            odd.append(jnp.where(half, pltpu.roll(a, 4, 0), b))
        last = first + 8 * len(even)
        send_ref[2 * t, first:last] = jnp.concatenate(even, axis=0).astype(jnp.bfloat16)
        send_ref[2 * t + 1, first:last] = jnp.concatenate(odd, axis=0).astype(jnp.bfloat16)


def kernel(
    h_ref, ids_hbm, mask_hbm, k1_hbm, k2_hbm, w_hbm,
    out_ref, dk1_hbm, dk2_hbm,
    ids_ref, mask_ref, w_ref, dk1_ref, dk2_ref, k1, k2, hv, x0, x1, tsend, tgot, perm, w8, acc, wide,
    act1, slope1, norm1, inv1, slope2, stat,
    hsend0, hsend1, ht0, ht1, d1, d2, dpad1, dpad2,
    psend1, psend2, pgot1, pgot2, rsend, rgot,
    gsend, ggot, rest2, zsend, zgot, final,
    send_sems, recv_sems, local_sems, ready_y, ready_x,
):
    f32, bf16 = jnp.float32, jnp.bfloat16
    s, m = lax.axis_index("seq"), lax.axis_index("mp")
    z = s // (XN * YN)
    xl = lax.rem(s // YN, XN)
    y = lax.rem(s, YN)
    seq_of = lambda z, x, y: (z * XN + x) * YN + y

    zs = Group((z,), (ZN,), lambda c: (seq_of(c[0], xl, y), m))
    ms = Group((m,), (MN,), lambda c: (s, c[0]))
    ys = Group((y,), (YN,), lambda c: (seq_of(z, xl, c[0]), m))
    xs = Group((xl,), (XN,), lambda c: (seq_of(z, c[0], y), m))
    core, xh = lax.rem(m, 2), m // 2
    cs = Group((core,), (2,), lambda c: (s, xh * 2 + c[0]))
    zx = Group((z, xh), (ZN, 2), lambda c: (seq_of(c[0], xl, y), c[1] * 2 + core))
    if MODE == "cube":
        z1, y1 = lax.rem(z, 2), lax.rem(y, 2)
        z2, y2 = z // 2, y // 2
        ga = Group((z1, xl, y1), (2, 2, 2), lambda c: (seq_of(z2 * 2 + c[0], c[1], y2 * 2 + c[2]), m))
        gb = Group((z2, y2), (4, 4), lambda c: (seq_of(c[0] * 2 + z1, xl, c[1] * 2 + y1), m))
        seq_at = lambda a, b: seq_of((b >> 2) * 2 + (a >> 2), (a >> 1) & 1, (b & 3) * 2 + (a & 1))
    else:
        ga = Group((z,), (ZN,), lambda c: (seq_of(c[0], xl, y), m))
        gb = Group((xl, y), (XN, YN), lambda c: (seq_of(z, c[0], c[1]), m))
        seq_at = lambda a, b: a * BN + b

    count = itertools.count()
    started = []

    class Exchange:
        def __init__(self, group, bytes_of_all):
            self.group, self.i = group, next(count)
            self.all = self.copy(bytes_of_all, bytes_of_all, group.to(group.offsets[0])[1])

        def copy(self, src, dst, device):
            return pltpu.make_async_remote_copy(
                src_ref=src, dst_ref=dst, send_sem=send_sems.at[self.i], recv_sem=recv_sems.at[self.i],
                device_id=device, device_id_type=MESH,
            )

        def start(self, src_of, dst_of):
            for off in self.group.offsets:
                to, device = self.group.to(off)
                self.copy(src_of(to), dst_of(self.group.me()), device).start()
            if self not in started:
                started.append(self)

        def start_one(self, off, src, dst):
            self.copy(src, dst, self.group.to(off)[1]).start()
            if self not in started:
                started.append(self)

        def wait(self):
            self.all.wait_recv()

        def wait_send(self):
            self.all.wait_send()

    rows16 = lambda i: pl.ds(pl.multiple_of(i * RES, RES), RES)
    lanes = lambda i: pl.ds(pl.multiple_of(i * 128, 128), 128)
    slices = lambda i: pl.ds(pl.multiple_of(i * SLICE, SLICE), SLICE)

    barrier = pltpu.get_barrier_semaphore()
    seen = 0
    for group in (zs, ys, ms, xs):
        for off in group.offsets:
            pl.semaphore_signal(barrier, inc=1, device_id=group.to(off)[1], device_id_type=MESH)
            seen += 1

    load_h = pltpu.make_async_copy(h_ref, hv, local_sems.at[0])
    load_k1 = pltpu.make_async_copy(k1_hbm, k1, local_sems.at[1])
    load_k2 = pltpu.make_async_copy(k2_hbm, k2, local_sems.at[2])
    load_ids = pltpu.make_async_copy(ids_hbm, ids_ref, local_sems.at[4])
    load_mask = pltpu.make_async_copy(mask_hbm, mask_ref, local_sems.at[5])
    load_w = pltpu.make_async_copy(w_hbm, w_ref, local_sems.at[6])
    load_h.start()
    load_k1.start()
    load_ids.start()
    load_mask.start()
    load_w.start()
    load_k2.start()

    load_h.wait()
    pl.semaphore_wait(barrier, seen)

    move_h = Exchange(zs, x0.at[pl.ds(0, ROWS - RES)])
    move_h.start(lambda to: hv.at[rows16(to)], lambda me: x0.at[rows16(me)])
    x0[rows16(z), :] = hv[rows16(z), :]
    for off in ys.offsets:
        pl.semaphore_signal(ready_y, inc=1, device_id=ys.to(off)[1], device_id_type=MESH)

    load_ids.wait()
    load_mask.wait()
    lane = lax.broadcasted_iota(jnp.int32, (8, 128), 1)
    sub = lax.broadcasted_iota(jnp.int32, (8, 128), 0)
    position = lane + s * ROWS
    hit = position == mask_ref[0]
    for q in range(1, 16):
        hit = jnp.logical_or(hit, position == mask_ref[q])
    target = jnp.where(hit, jnp.broadcast_to(ids_ref[...], (8, 128)), -1).astype(f32)
    target = pltpu.roll(target, z * RES, 1)
    tsend[...] = target
    row = lambda i: pl.ds(i, 1)
    move_t = Exchange(zs, tgot.at[pl.ds(0, ZN - 1)])
    move_t.start(lambda to: tsend.at[row(0)], lambda me: tgot.at[row(me)])
    tgot[row(z), :] = target[0:1]

    p = lax.broadcasted_iota(jnp.int32, (CH, 128), 0)
    a, b, low = p >> 6, (p >> 2) & (BN - 1), p & 3
    channel = seq_at(a, b) * 4 + low - lax.broadcasted_iota(jnp.int32, (CH, 128), 1)
    for i in range(CH // 128):
        perm[:, i * 128 : i * 128 + 128] = (channel == i * 128).astype(f32).astype(bf16)

    load_w.wait()
    w8[...] = jnp.concatenate([w_ref[...].astype(f32), jnp.zeros((8 - VOCAB, CH), f32)], axis=0)
    for dpad, halo in ((dpad1, HALO1), (dpad2, HALO2)):
        zero = jnp.zeros((AN, halo, RES, OWN), bf16)
        dpad[:, 0:halo] = zero
        dpad[:, halo + ZN : 2 * halo + ZN] = zero

    load_k1.wait()
    move_h.wait()

    conv(x0, k1, HOP1, REACH1, acc)
    activation, slope = gelu_parts(acc[...])
    slope1[...] = slope
    act1[m] = activation.astype(bf16)
    gather1 = Exchange(ms, act1.at[pl.ds(0, MN - 1)])
    gather1.start(lambda to: act1.at[m], lambda me: act1.at[me])

    pl.semaphore_wait(ready_y, YN - 1)
    pl.semaphore_signal(ready_x, inc=1, device_id=xs.to((1,))[1], device_id_type=MESH)

    mine = ga.me()
    hsend0[...] = nt(perm[...], x0[...]).astype(bf16)
    ht0[:, lanes(mine)] = hsend0[slices(mine), :]
    pl.semaphore_wait(ready_x, XN - 1)
    move0 = Exchange(ga, ht0.at[:, pl.ds(0, (AN - 1) * ROWS)])
    move0.start(lambda to: hsend0.at[slices(to)], lambda me: ht0.at[:, lanes(me)])
    move_t.wait()
    load_k2.wait()
    gather1.wait()

    values = jnp.concatenate([act1[i] for i in range(MN)], axis=1).astype(f32)
    centred = values - jnp.mean(values, axis=1, keepdims=True)
    inverse = lax.rsqrt(jnp.mean(centred * centred, axis=1, keepdims=True) + epsilon)
    normed = centred * inverse
    for i in range(MN):
        norm1[i] = normed[:, i * 128 : i * 128 + 128]
    inv1[...] = jnp.broadcast_to(inverse, (ROWS, 128))
    x1[...] = (x0[...].astype(f32) + normed).astype(bf16)

    conv(x1, k2, HOP2, REACH2, acc)
    activation, slope = gelu_parts(acc[...])
    slope2[...] = slope
    act2 = activation.astype(bf16)
    values2 = act2.astype(f32)
    w_own = w8[:, lanes(m)]
    sub_own = lax.broadcasted_iota(jnp.int32, (8, OWN), 0)
    left = jnp.where(sub_own == VOCAB, 1.0, w_own).astype(bf16)
    ones = jnp.ones((8, OWN), bf16)
    off_mean = values2 - jnp.mean(values2, axis=1, keepdims=True)
    sums = nt(left, act2)
    squares = split_dot(ones, off_mean * off_mean)
    stat[m] = jnp.where(sub == VOCAB + 1, squares, sums)
    share = Exchange(ms, stat.at[pl.ds(0, MN - 1)])
    share.start(lambda to: stat.at[m], lambda me: stat.at[me])

    hsend1[...] = nt(perm[...], x1[...]).astype(bf16)
    ht1[:, lanes(mine)] = hsend1[slices(mine), :]
    move1 = Exchange(ga, ht1.at[:, pl.ds(0, (AN - 1) * ROWS)])
    move1.start(lambda to: hsend1.at[slices(to)], lambda me: ht1.at[:, lanes(me)])
    own_logits = nt(w8[...].astype(bf16), x1[...])
    w_sum = jnp.sum(w8[...], axis=1, keepdims=True)
    turned = pltpu.roll(tgot[...], lax.rem(ROWS - z * RES, ROWS), 1)
    targets = jnp.sum(jnp.where(lane // RES == sub, turned, 0.0), axis=0, keepdims=True)
    share.wait()

    each = [stat[i] for i in range(MN)]
    total = each[0] + each[1] + each[2] + each[3]
    mean2 = total[VOCAB : VOCAB + 1] * (1.0 / CH)
    spread = total[VOCAB + 1 : VOCAB + 2]
    for part in each:
        apart = part[VOCAB : VOCAB + 1] * (1.0 / OWN) - mean2
        spread = spread + OWN * apart * apart
    inv2 = lax.rsqrt(spread * (1.0 / CH) + epsilon)
    along = inv2 * (total - mean2 * w_sum)
    logits = own_logits + along
    classes = sub < VOCAB
    exponent = jnp.where(classes, jnp.exp(logits), 0.0)
    probability = exponent / jnp.sum(exponent, axis=0, keepdims=True)
    onehot = (sub.astype(f32) == targets).astype(f32)
    dlogits = jnp.where(jnp.logical_and(classes, targets >= 0.0), probability - onehot, 0.0)
    mean_grad = jnp.sum(dlogits * w_sum, axis=0, keepdims=True) * (1.0 / CH)
    mean_cross = jnp.sum(jnp.where(classes, dlogits * along, 0.0), axis=0, keepdims=True) * (1.0 / CH)
    slant = inv2 * mean_cross
    shift = mean_grad - slant * mean2
    packed = jnp.where(sub == 5, inv2, jnp.where(sub == 6, shift, jnp.where(sub == 7, slant, dlogits)))
    by_row = jnp.transpose(jnp.concatenate([packed, jnp.zeros((ROWS - 8, 128), f32)], axis=0))
    grad2 = by_row[:, 0:1] * w_own[0:1]
    for v in range(1, VOCAB):
        grad2 = grad2 + by_row[:, v : v + 1] * w_own[v : v + 1]
    dconv = by_row[:, 5:6] * (grad2 - by_row[:, 6:7] - values2 * by_row[:, 7:8]) * slope2[...]
    dconv = dconv.astype(bf16)
    d2[...] = dconv
    dpad2[mine, HALO2 : HALO2 + ZN] = dconv.reshape(ZN, RES, OWN)

    share2 = Exchange(ga, dpad2.at[pl.ds(0, AN - 1), pl.ds(HALO2, ZN)])
    share2.start(lambda to: dpad2.at[mine, pl.ds(HALO2, ZN)], lambda me: dpad2.at[me, pl.ds(HALO2, ZN)])

    first = grad2
    second = grad2 * norm1[m]
    reduce2 = Exchange(ms, pgot2.at[pl.ds(0, MN - 1)])
    for step in (2, 3, 1, 0):
        i = lax.rem(m + step, MN)
        back_conv_part(d2, k2, HOP2, REACH2, i, acc)
        part = acc[...].astype(bf16)
        if step:
            psend2[i] = part
            reduce2.start_one((step,), psend2.at[i], pgot2.at[m])
        else:
            pgot2[m] = part
        part = part.astype(f32)
        first = first + part
        second = second + part * norm1[i]
    rows_sum = jnp.where(sub == 0, split_dot(ones, first), split_dot(ones, second))
    rsend[...] = rows_sum
    rgot[m] = rows_sum
    reduce_rows = Exchange(ms, rgot.at[pl.ds(0, MN - 1)])
    reduce_rows.start(lambda to: rsend, lambda me: rgot.at[me])

    reduce2.wait()
    reduce_rows.wait()
    grad1 = grad2
    for i in range(MN):
        grad1 = grad1 + pgot2[i].astype(f32)
    rows_sum = (rgot[0] + rgot[1] + rgot[2] + rgot[3]) * (1.0 / CH)
    by_row = jnp.transpose(jnp.concatenate([rows_sum, jnp.zeros((ROWS - 8, 128), f32)], axis=0))
    dconv = inv1[...] * (grad1 - by_row[:, 0:1] - norm1[m] * by_row[:, 1:2]) * slope1[...]
    dconv = dconv.astype(bf16)
    d1[...] = dconv
    dpad1[mine, HALO1 : HALO1 + ZN] = dconv.reshape(ZN, RES, OWN)
    share1 = Exchange(ga, dpad1.at[pl.ds(0, AN - 1), pl.ds(HALO1, ZN)])
    share1.start(lambda to: dpad1.at[mine, pl.ds(HALO1, ZN)], lambda me: dpad1.at[me, pl.ds(HALO1, ZN)])

    back_conv(d1, k1, HOP1, REACH1, wide)
    for c in range(2):
        for i in range(2):
            at = (i * 2 + c) * 128
            psend1[c, i] = wide[:, at : at + 128].astype(bf16)
    reduce1 = Exchange(cs, pgot1)
    reduce1.start(lambda to: psend1.at[to], lambda me: pgot1)
    wide[:, lanes(m)] += grad1

    move1.wait()
    share2.wait()
    owner = gb.me()
    grads = tap_gradients(ht1, dpad2, HOP2, REACH2, HALO2)
    pieces(grads[:4], gsend, 0)
    for i in range(3):
        rest2[i] = grads[4 + i]

    reduce1.wait()
    for i in range(2):
        zsend[i] = (wide[:, lanes(i * 2 + core)] + pgot1[i].astype(f32)).astype(bf16)
    zgot[zx.me()] = zsend[:, rows16(z), :]
    move_back = Exchange(zx, zgot.at[pl.ds(0, 2 * ZN - 1)])
    move_back.start(lambda to: zsend.at[:, rows16(to // 2)], lambda me: zgot.at[me])

    move0.wait()
    share1.wait()
    grads = tap_gradients(ht0, dpad1, HOP1, REACH1, HALO1)
    pieces([rest2[i] for i in range(3)] + grads, gsend, 16)
    ggot[owner] = gsend[owner]
    scatter = Exchange(gb, ggot.at[pl.ds(0, BN - 1)])
    scatter.start(lambda to: gsend.at[to], lambda me: ggot.at[me])

    move_back.wait()
    gather_out = Exchange(cs, out_ref.at[:, pl.ds(0, 2 * OWN)])
    keep = []
    for i in range(2):
        for r in range(ZN):
            total = zgot[2 * r, i].astype(f32) + zgot[2 * r + 1, i].astype(f32)
            final[i, r * RES : r * RES + RES] = total.astype(bf16)
        place = out_ref.at[:, lanes(i * 2 + core)]
        keep.append(pltpu.make_async_copy(final.at[i], place, local_sems.at[3 + 6 * i]))
        keep[i].start()
        gather_out.start(lambda to: final.at[i], lambda me: place)

    dk2_ref[0] = jnp.zeros((4, OWN), f32)
    dk2_ref[TAPS - 1] = jnp.zeros((4, OWN), f32)
    scatter.wait()
    grads = ggot[0].astype(f32)
    for i in range(1, BN):
        grads = grads + ggot[i].astype(f32)
    for j in range(2 * REACH2 + 1):
        dk2_ref[MID - REACH2 + j] = grads[4 * j : 4 * j + 4]
    for j in range(TAPS):
        dk1_ref[j] = grads[28 + 4 * j : 32 + 4 * j]
    store2 = pltpu.make_async_copy(dk2_ref, dk2_hbm, local_sems.at[7])
    store1 = pltpu.make_async_copy(dk1_ref, dk1_hbm, local_sems.at[8])
    store2.start()
    store1.start()

    gather_out.wait()
    for copy in keep:
        copy.wait()
    store2.wait()
    store1.wait()
    for exchange in started:
        exchange.wait_send()


def local(h, ids, mask_index, k1, k2, w):
    f32, bf16 = jnp.float32, jnp.bfloat16
    vmem = pltpu.VMEM
    hbm = pl.BlockSpec(memory_space=pltpu.HBM)
    copies = 15
    operands = (h, ids.reshape(1, ROWS), mask_index, k1, k2, w.T)
    return pl.pallas_call(
        kernel,
        out_shape=(
            jax.ShapeDtypeStruct((ROWS, CH), bf16),
            jax.ShapeDtypeStruct((TAPS, 4, OWN), f32),
            jax.ShapeDtypeStruct((TAPS, 4, OWN), f32),
        ),
        in_specs=[hbm] * 6,
        out_specs=(hbm, hbm, hbm),
        scratch_shapes=[
            vmem((1, ROWS), jnp.int32),
            pltpu.SMEM((16,), jnp.int32),
            vmem((VOCAB, CH), bf16),
            vmem((TAPS, 4, OWN), f32),
            vmem((TAPS, 4, OWN), f32),
            vmem((TAPS, CH, OWN), bf16),
            vmem((TAPS, CH, OWN), bf16),
            vmem((ROWS, CH), bf16),
            vmem((ROWS, CH), bf16),
            vmem((ROWS, CH), bf16),
            vmem((8, 128), f32),
            vmem((ZN, 128), f32),
            vmem((CH, CH), bf16),
            vmem((8, CH), f32),
            vmem((ROWS, OWN), f32),
            vmem((ROWS, CH), f32),
            vmem((MN, ROWS, OWN), bf16),
            vmem((ROWS, OWN), f32),
            vmem((MN, ROWS, OWN), f32),
            vmem((ROWS, 128), f32),
            vmem((ROWS, OWN), f32),
            vmem((MN, 8, 128), f32),
            vmem((CH, ROWS), bf16),
            vmem((CH, ROWS), bf16),
            vmem((SLICE, AN * ROWS), bf16),
            vmem((SLICE, AN * ROWS), bf16),
            vmem((ROWS, OWN), bf16),
            vmem((ROWS, OWN), bf16),
            vmem((AN, ZN + 2 * HALO1, RES, OWN), bf16),
            vmem((AN, ZN + 2 * HALO2, RES, OWN), bf16),
            vmem((2, 2, ROWS, OWN), bf16),
            vmem((MN, ROWS, OWN), bf16),
            vmem((2, ROWS, OWN), bf16),
            vmem((MN, ROWS, OWN), bf16),
            vmem((8, 128), f32),
            vmem((MN, 8, 128), f32),
            vmem((BN, PIECE, OWN), bf16),
            vmem((BN, PIECE, OWN), bf16),
            vmem((3, SLICE, OWN), f32),
            vmem((2, ROWS, OWN), bf16),
            vmem((2 * ZN, 2, RES, OWN), bf16),
            vmem((2, ROWS, OWN), bf16),
            pltpu.SemaphoreType.DMA((copies,)),
            pltpu.SemaphoreType.DMA((copies,)),
            pltpu.SemaphoreType.DMA((10,)),
            pltpu.SemaphoreType.REGULAR,
            pltpu.SemaphoreType.REGULAR,
        ],
        compiler_params=pltpu.CompilerParams(
            collective_id=0, has_side_effects=True, vmem_limit_bytes=40 * 1024 * 1024
        ),
    )(*(pltpu.with_memory_space_constraint(v, pltpu.HBM) for v in operands))


def solution(mesh):
    placed = (P("seq", None), P("seq"), P("seq"), P(None, None, "mp"), P(None, None, "mp"), P())
    return jax.shard_map(
        local,
        mesh=mesh,
        in_specs=placed,
        out_specs=(P("seq", None), P(None, "seq", "mp"), P(None, "seq", "mp")),
        check_vma=False,
    )
```

```python
import functools
import itertools

import jax
import jax.numpy as jnp
from jax import lax
from jax.experimental import pallas as pl
from jax.experimental.pallas import tpu as pltpu
from jax.sharding import PartitionSpec as P

MESH = pl.DeviceIdType.MESH
ZN, XN, YN, MN = 8, 2, 8, 4
ROWS, CH, OWN, TAPS, VOCAB = 128, 512, 128, 9, 5
RES = ROWS // ZN
MID = TAPS // 2
HOP1, HOP2 = 1, 2
REACH1, REACH2 = 4, 3
HALO1, HALO2 = REACH1 * HOP1, REACH2 * HOP2
PIECE1, PIECE2 = 48, 32
AN, BN = 8, 16
SLICE = CH // AN

epsilon = 1e-05
root_half = 0.7071067811865476
inv_root_two_pi = 0.3989422804014327


def nn(a, b):
    return lax.dot_general(a, b, (((1,), (0,)), ((), ())), preferred_element_type=jnp.float32)


def nt(a, b):
    return lax.dot_general(a, b, (((1,), (1,)), ((), ())), preferred_element_type=jnp.float32)


def split_dot(left, values):
    high = values.astype(jnp.bfloat16)
    low = (values - high.astype(jnp.float32)).astype(jnp.bfloat16)
    return nt(left, high) + nt(left, low)


def gelu_parts(conv_out):
    normal_cdf = 0.5 * (1.0 + lax.erf(conv_out * root_half))
    slope = normal_cdf + conv_out * inv_root_two_pi * jnp.exp(-0.5 * conv_out * conv_out)
    return conv_out * normal_cdf, slope


class Group:
    def __init__(self, coords, mods, place):
        self.coords, self.mods, self.place = coords, mods, place
        every = itertools.product(*(range(n) for n in mods))
        distance = lambda off: sum(min(o, n - o) for o, n in zip(off, mods))
        self.offsets = sorted((o for o in every if any(o)), key=lambda o: -distance(o))

    def moved(self, off, back):
        return tuple(
            c if o == 0 else lax.rem(c + (n - o if back else o), n)
            for c, o, n in zip(self.coords, off, self.mods)
        )

    def index(self, coords):
        at = coords[0]
        for c, n in zip(coords[1:], self.mods[1:]):
            at = at * n + c
        return at

    def me(self):
        return self.index(self.coords)

    def to(self, off):
        coords = self.moved(off, False)
        return self.index(coords), self.place(coords)

    def source(self, off):
        return self.index(self.moved(off, True))


def conv(x_ref, k_ref, hop, reach, acc_ref):
    acc_ref[...] = nn(x_ref[...], k_ref[MID])
    for j in range(-reach, reach + 1):
        if j == 0:
            continue
        n = (ZN - abs(j) * hop) * RES
        to = max(0, -j * hop) * RES
        at = max(0, j * hop) * RES
        acc_ref[to : to + n, :] += nn(x_ref[at : at + n, :], k_ref[MID + j])


def back_conv(d_ref, k_ref, hop, reach, acc_ref):
    acc_ref[...] = nt(d_ref[...], k_ref[MID])
    for j in range(-reach, reach + 1):
        if j == 0:
            continue
        n = (ZN - abs(j) * hop) * RES
        to = max(0, j * hop) * RES
        at = max(0, -j * hop) * RES
        acc_ref[to : to + n, :] += nt(d_ref[at : at + n, :], k_ref[MID + j])


def back_conv_part(d_ref, k_ref, hop, reach, part, acc_ref):
    channels = pl.ds(pl.multiple_of(part * OWN, OWN), OWN)
    acc_ref[...] = nt(d_ref[...], k_ref[MID, channels, :])
    for j in range(-reach, reach + 1):
        if j == 0:
            continue
        n = (ZN - abs(j) * hop) * RES
        to = max(0, j * hop) * RES
        at = max(0, -j * hop) * RES
        acc_ref[to : to + n, :] += nt(d_ref[at : at + n, :], k_ref[MID + j, channels, :])


def tap_gradients(ht_ref, d_ref, hop, reach, halo):
    left = ht_ref[...]
    out = []
    for j in range(-reach, reach + 1):
        at = halo - j * hop
        right = d_ref[:, at : at + ZN, :, :].reshape(AN * ROWS, OWN)
        out.append(nn(left, right))
    return out


def pieces(grads, send_ref, first):
    half = lax.broadcasted_iota(jnp.int32, (8, OWN), 0) < 4
    for t in range(SLICE // 8):
        even, odd = [], []
        for a, b in zip(grads[::2], grads[1::2]):
            a, b = a[8 * t : 8 * t + 8], b[8 * t : 8 * t + 8]
            even.append(jnp.where(half, a, pltpu.roll(b, 4, 0)))
            odd.append(jnp.where(half, pltpu.roll(a, 4, 0), b))
        last = first + 8 * len(even)
        send_ref[2 * t, first:last] = jnp.concatenate(even, axis=0).astype(jnp.bfloat16)
        send_ref[2 * t + 1, first:last] = jnp.concatenate(odd, axis=0).astype(jnp.bfloat16)


def kernel(
    h_ref, ids_hbm, mask_hbm, k1_hbm, k2_hbm, w_hbm,
    out_ref, dk1_ref, dk2_ref,
    ids_ref, mask_ref, w_ref, k1, k2, hv, x0, x1, tsend, tgot, perm, w8, acc, wide,
    act1, slope1, norm1, inv1, slope2, stat,
    hsend0, hsend1, ht0, ht1, d1, d2, dpad1, dpad2,
    psend1, psend2, pgot1, pgot2, rsend, rgot,
    gsend, ggot, gsend2, ggot2, perm2, zsend, zgot, final,
    send_sems, recv_sems, local_sems, ready_x,
):
    f32, bf16 = jnp.float32, jnp.bfloat16
    s, m = lax.axis_index("seq"), lax.axis_index("mp")
    z = s // (XN * YN)
    xl = lax.rem(s // YN, XN)
    y = lax.rem(s, YN)
    seq_of = lambda z, x, y: (z * XN + x) * YN + y

    zs = Group((z,), (ZN,), lambda c: (seq_of(c[0], xl, y), m))
    ms = Group((m,), (MN,), lambda c: (s, c[0]))
    ys = Group((y,), (YN,), lambda c: (seq_of(z, xl, c[0]), m))
    xs = Group((xl,), (XN,), lambda c: (seq_of(z, c[0], y), m))
    core, xh = lax.rem(m, 2), m // 2
    cs = Group((core,), (2,), lambda c: (s, xh * 2 + c[0]))
    zx = Group((z, xh), (ZN, 2), lambda c: (seq_of(c[0], xl, y), c[1] * 2 + core))
    ga = ys
    gb = Group((z, xl), (ZN, XN), lambda c: (seq_of(c[0], c[1], y), m))
    gb2 = Group((xl, y), (XN, YN), lambda c: (seq_of(z, c[0], c[1]), m))
    seq_at = lambda a, b: seq_of(b >> 1, b & 1, a)

    count = itertools.count()
    started = []

    class Exchange:
        def __init__(self, group, bytes_of_all):
            self.group, self.i = group, next(count)
            self.all = self.copy(bytes_of_all, bytes_of_all, group.to(group.offsets[0])[1])

        def copy(self, src, dst, device):
            return pltpu.make_async_remote_copy(
                src_ref=src, dst_ref=dst, send_sem=send_sems.at[self.i], recv_sem=recv_sems.at[self.i],
                device_id=device, device_id_type=MESH,
            )

        def start(self, src_of, dst_of, chosen=lambda off: True):
            for off in filter(chosen, self.group.offsets):
                to, device = self.group.to(off)
                self.copy(src_of(to), dst_of(self.group.me()), device).start()
            if self not in started:
                started.append(self)

        def start_one(self, off, src, dst):
            self.copy(src, dst, self.group.to(off)[1]).start()
            if self not in started:
                started.append(self)

        def wait(self):
            self.all.wait_recv()

        def wait_send(self):
            self.all.wait_send()

    rows16 = lambda i: pl.ds(pl.multiple_of(i * RES, RES), RES)
    lanes = lambda i: pl.ds(pl.multiple_of(i * 128, 128), 128)
    slices = lambda i: pl.ds(pl.multiple_of(i * SLICE, SLICE), SLICE)

    barrier = pltpu.get_barrier_semaphore()
    seen = 0
    for group in (zs, ys, ms, xs):
        for off in group.offsets:
            pl.semaphore_signal(barrier, inc=1, device_id=group.to(off)[1], device_id_type=MESH)
            seen += 1

    load_h = pltpu.make_async_copy(h_ref, hv, local_sems.at[0])
    load_k1 = pltpu.make_async_copy(k1_hbm, k1, local_sems.at[1])
    load_k2 = pltpu.make_async_copy(k2_hbm, k2, local_sems.at[2])
    load_ids = pltpu.make_async_copy(ids_hbm, ids_ref, local_sems.at[4])
    load_mask = pltpu.make_async_copy(mask_hbm, mask_ref, local_sems.at[5])
    load_w = pltpu.make_async_copy(w_hbm, w_ref, local_sems.at[6])
    load_h.start()
    load_k1.start()
    load_ids.start()
    load_mask.start()
    load_w.start()
    load_k2.start()

    load_h.wait()
    pl.semaphore_wait(barrier, seen)

    move_h = Exchange(zs, x0.at[pl.ds(0, ROWS - RES)])
    move_h.start(lambda to: hv.at[rows16(to)], lambda me: x0.at[rows16(me)])
    x0[rows16(z), :] = hv[rows16(z), :]
    pl.semaphore_signal(ready_x, inc=1, device_id=xs.to((1,))[1], device_id_type=MESH)

    load_ids.wait()
    load_mask.wait()
    lane = lax.broadcasted_iota(jnp.int32, (8, 128), 1)
    sub = lax.broadcasted_iota(jnp.int32, (8, 128), 0)
    position = lane + s * ROWS
    hit = position == mask_ref[0]
    for q in range(1, 16):
        hit = jnp.logical_or(hit, position == mask_ref[q])
    target = jnp.where(hit, jnp.broadcast_to(ids_ref[...], (8, 128)), -1).astype(f32)
    target = pltpu.roll(target, z * RES, 1)
    tsend[...] = target
    row = lambda i: pl.ds(i, 1)
    move_t = Exchange(zs, tgot.at[pl.ds(0, ZN - 1)])
    move_t.start(lambda to: tsend.at[row(0)], lambda me: tgot.at[row(me)])
    tgot[row(z), :] = target[0:1]

    p = lax.broadcasted_iota(jnp.int32, (CH, 128), 0)
    a, b, low = p >> 6, (p >> 2) & (BN - 1), p & 3
    channel = seq_at(a, b) * 4 + low - lax.broadcasted_iota(jnp.int32, (CH, 128), 1)
    same = p - lax.broadcasted_iota(jnp.int32, (CH, 128), 1)
    for i in range(CH // 128):
        perm[:, i * 128 : i * 128 + 128] = (channel == i * 128).astype(f32).astype(bf16)
        perm2[:, i * 128 : i * 128 + 128] = (same == i * 128).astype(f32).astype(bf16)

    load_w.wait()
    w8[...] = jnp.concatenate([w_ref[...].astype(f32), jnp.zeros((8 - VOCAB, CH), f32)], axis=0)
    for dpad, halo in ((dpad1, HALO1), (dpad2, HALO2)):
        zero = jnp.zeros((AN, halo, RES, OWN), bf16)
        dpad[:, 0:halo] = zero
        dpad[:, halo + ZN : 2 * halo + ZN] = zero

    load_k1.wait()
    move_h.wait()

    conv(x0, k1, HOP1, REACH1, acc)
    activation, slope = gelu_parts(acc[...])
    slope1[...] = slope
    act1[m] = activation.astype(bf16)
    gather1 = Exchange(ms, act1.at[pl.ds(0, MN - 1)])
    gather1.start(lambda to: act1.at[m], lambda me: act1.at[me])

    mine = ga.me()
    hsend0[...] = nt(perm[...], x0[...]).astype(bf16)
    ht0[:, lanes(mine)] = hsend0[slices(mine), :]
    move0 = Exchange(ga, ht0.at[:, pl.ds(0, (AN - 1) * ROWS)])
    move0.start(lambda to: hsend0.at[slices(to)], lambda me: ht0.at[:, lanes(me)])
    move_t.wait()
    load_k2.wait()
    gather1.wait()

    values = jnp.concatenate([act1[i] for i in range(MN)], axis=1).astype(f32)
    centred = values - jnp.mean(values, axis=1, keepdims=True)
    inverse = lax.rsqrt(jnp.mean(centred * centred, axis=1, keepdims=True) + epsilon)
    normed = centred * inverse
    for i in range(MN):
        norm1[i] = normed[:, i * 128 : i * 128 + 128]
    inv1[...] = jnp.broadcast_to(inverse, (ROWS, 128))
    x1[...] = (x0[...].astype(f32) + normed).astype(bf16)

    conv(x1, k2, HOP2, REACH2, acc)
    activation, slope = gelu_parts(acc[...])
    slope2[...] = slope
    act2 = activation.astype(bf16)
    values2 = act2.astype(f32)
    w_own = w8[:, lanes(m)]
    sub_own = lax.broadcasted_iota(jnp.int32, (8, OWN), 0)
    left = jnp.where(sub_own == VOCAB, 1.0, w_own).astype(bf16)
    ones = jnp.ones((8, OWN), bf16)
    off_mean = values2 - jnp.mean(values2, axis=1, keepdims=True)
    sums = nt(left, act2)
    squares = split_dot(ones, off_mean * off_mean)
    stat[m] = jnp.where(sub == VOCAB + 1, squares, sums)
    share = Exchange(ms, stat.at[pl.ds(0, MN - 1)])
    share.start(lambda to: stat.at[m], lambda me: stat.at[me])

    hsend1[...] = nt(perm2[...], x1[...]).astype(bf16)
    ht1[:, lanes(z)] = hsend1[slices(z), :]
    move1 = Exchange(zs, ht1.at[:, pl.ds(0, (AN - 1) * ROWS)])
    move1.start(lambda to: hsend1.at[slices(to)], lambda me: ht1.at[:, lanes(me)])
    own_logits = nt(w8[...].astype(bf16), x1[...])
    w_sum = jnp.sum(w8[...], axis=1, keepdims=True)
    turned = pltpu.roll(tgot[...], lax.rem(ROWS - z * RES, ROWS), 1)
    targets = jnp.sum(jnp.where(lane // RES == sub, turned, 0.0), axis=0, keepdims=True)
    share.wait()

    each = [stat[i] for i in range(MN)]
    total = each[0] + each[1] + each[2] + each[3]
    mean2 = total[VOCAB : VOCAB + 1] * (1.0 / CH)
    spread = total[VOCAB + 1 : VOCAB + 2]
    for part in each:
        apart = part[VOCAB : VOCAB + 1] * (1.0 / OWN) - mean2
        spread = spread + OWN * apart * apart
    inv2 = lax.rsqrt(spread * (1.0 / CH) + epsilon)
    along = inv2 * (total - mean2 * w_sum)
    logits = own_logits + along
    classes = sub < VOCAB
    exponent = jnp.where(classes, jnp.exp(logits), 0.0)
    probability = exponent / jnp.sum(exponent, axis=0, keepdims=True)
    onehot = (sub.astype(f32) == targets).astype(f32)
    dlogits = jnp.where(jnp.logical_and(classes, targets >= 0.0), probability - onehot, 0.0)
    mean_grad = jnp.sum(dlogits * w_sum, axis=0, keepdims=True) * (1.0 / CH)
    mean_cross = jnp.sum(jnp.where(classes, dlogits * along, 0.0), axis=0, keepdims=True) * (1.0 / CH)
    slant = inv2 * mean_cross
    shift = mean_grad - slant * mean2
    packed = jnp.where(sub == 5, inv2, jnp.where(sub == 6, shift, jnp.where(sub == 7, slant, dlogits)))
    by_row = jnp.transpose(jnp.concatenate([packed, jnp.zeros((ROWS - 8, 128), f32)], axis=0))
    grad2 = by_row[:, 0:1] * w_own[0:1]
    for v in range(1, VOCAB):
        grad2 = grad2 + by_row[:, v : v + 1] * w_own[v : v + 1]
    dconv = by_row[:, 5:6] * (grad2 - by_row[:, 6:7] - values2 * by_row[:, 7:8]) * slope2[...]
    dconv = dconv.astype(bf16)
    d2[...] = dconv
    dpad2[z, HALO2 : HALO2 + ZN] = dconv.reshape(ZN, RES, OWN)

    share2 = Exchange(zs, dpad2.at[pl.ds(0, AN - 1), pl.ds(HALO2, ZN)])
    share2.start(lambda to: dpad2.at[z, pl.ds(HALO2, ZN)], lambda me: dpad2.at[me, pl.ds(HALO2, ZN)])

    first = grad2
    second = grad2 * norm1[m]
    reduce2 = Exchange(ms, pgot2.at[pl.ds(0, MN - 1)])
    for step in (2, 3, 1, 0):
        i = lax.rem(m + step, MN)
        back_conv_part(d2, k2, HOP2, REACH2, i, acc)
        part = acc[...].astype(bf16)
        if step:
            psend2[i] = part
            reduce2.start_one((step,), psend2.at[i], pgot2.at[m])
        else:
            pgot2[m] = part
        part = part.astype(f32)
        first = first + part
        second = second + part * norm1[i]
    rows_sum = jnp.where(sub == 0, split_dot(ones, first), split_dot(ones, second))
    rsend[...] = rows_sum
    rgot[m] = rows_sum
    reduce_rows = Exchange(ms, rgot.at[pl.ds(0, MN - 1)])
    reduce_rows.start(lambda to: rsend, lambda me: rgot.at[me])

    reduce2.wait()
    reduce_rows.wait()
    grad1 = grad2
    for i in range(MN):
        grad1 = grad1 + pgot2[i].astype(f32)
    rows_sum = (rgot[0] + rgot[1] + rgot[2] + rgot[3]) * (1.0 / CH)
    by_row = jnp.transpose(jnp.concatenate([rows_sum, jnp.zeros((ROWS - 8, 128), f32)], axis=0))
    dconv = inv1[...] * (grad1 - by_row[:, 0:1] - norm1[m] * by_row[:, 1:2]) * slope1[...]
    dconv = dconv.astype(bf16)
    d1[...] = dconv
    dpad1[mine, HALO1 : HALO1 + ZN] = dconv.reshape(ZN, RES, OWN)
    share1 = Exchange(ga, dpad1.at[pl.ds(0, AN - 1), pl.ds(HALO1, ZN)])
    share1.start(lambda to: dpad1.at[mine, pl.ds(HALO1, ZN)], lambda me: dpad1.at[me, pl.ds(HALO1, ZN)])

    back_conv(d1, k1, HOP1, REACH1, wide)
    for c in range(2):
        for i in range(2):
            at = (i * 2 + c) * 128
            psend1[c, i] = wide[:, at : at + 128].astype(bf16)
    reduce1 = Exchange(cs, pgot1)
    reduce1.start(lambda to: psend1.at[to], lambda me: pgot1)
    wide[:, lanes(m)] += grad1

    move1.wait()
    share2.wait()
    owner, owner2 = gb.me(), gb2.me()
    nothing = jnp.zeros((SLICE, OWN), f32)
    pieces(tap_gradients(ht1, dpad2, HOP2, REACH2, HALO2) + [nothing], gsend2, 0)
    ggot2[owner2] = gsend2[owner2]
    pl.semaphore_wait(ready_x, XN - 1)
    scatter2 = Exchange(gb2, ggot2.at[pl.ds(0, BN - 1)])
    scatter2.start(lambda to: gsend2.at[to], lambda me: ggot2.at[me])

    reduce1.wait()
    for i in range(2):
        zsend[i] = (wide[:, lanes(i * 2 + core)] + pgot1[i].astype(f32)).astype(bf16)
    zgot[zx.me()] = zsend[:, rows16(z), :]
    move_back = Exchange(zx, zgot.at[pl.ds(0, 2 * ZN - 1)])
    move_back.start(lambda to: zsend.at[:, rows16(to // 2)], lambda me: zgot.at[me])

    move0.wait()
    share1.wait()
    pieces(tap_gradients(ht0, dpad1, HOP1, REACH1, HALO1) + [nothing] * 3, gsend, 0)
    ggot[owner] = gsend[owner]
    scatter = Exchange(gb, ggot.at[pl.ds(0, BN - 1)])
    scatter.start(lambda to: gsend.at[to], lambda me: ggot.at[me])

    move_back.wait()
    gather_out = Exchange(cs, out_ref.at[:, pl.ds(0, 2 * OWN)])
    keep = []
    for i in range(2):
        for r in range(ZN):
            total = zgot[2 * r, i].astype(f32) + zgot[2 * r + 1, i].astype(f32)
            final[i, r * RES : r * RES + RES] = total.astype(bf16)
        place = out_ref.at[:, lanes(i * 2 + core)]
        keep.append(pltpu.make_async_copy(final.at[i], place, local_sems.at[3 + 6 * i]))
        keep[i].start()
        gather_out.start(lambda to: final.at[i], lambda me: place)

    dk2_ref[0] = jnp.zeros((4, OWN), f32)
    dk2_ref[TAPS - 1] = jnp.zeros((4, OWN), f32)
    scatter2.wait()
    grads = ggot2[0].astype(f32)
    for i in range(1, BN):
        grads = grads + ggot2[i].astype(f32)
    for j in range(2 * REACH2 + 1):
        dk2_ref[MID - REACH2 + j] = grads[4 * j : 4 * j + 4]
    scatter.wait()
    grads = ggot[0].astype(f32)
    for i in range(1, BN):
        grads = grads + ggot[i].astype(f32)
    for j in range(TAPS):
        dk1_ref[j] = grads[4 * j : 4 * j + 4]

    gather_out.wait()
    for copy in keep:
        copy.wait()
    for exchange in started:
        exchange.wait_send()


def local(h, ids, mask_index, k1, k2, w):
    f32, bf16 = jnp.float32, jnp.bfloat16
    vmem = pltpu.VMEM
    inside = pl.BlockSpec(memory_space=pltpu.VMEM)
    hbm = pl.BlockSpec(memory_space=pltpu.HBM)
    copies = 15
    operands = (h, ids.reshape(1, ROWS), mask_index, k1, k2, w.T)
    return pl.pallas_call(
        kernel,
        out_shape=(
            jax.ShapeDtypeStruct((ROWS, CH), bf16),
            jax.ShapeDtypeStruct((TAPS, 4, OWN), f32),
            jax.ShapeDtypeStruct((TAPS, 4, OWN), f32),
        ),
        in_specs=[hbm] * 6,
        out_specs=(hbm, inside, inside),
        scratch_shapes=[
            vmem((1, ROWS), jnp.int32),
            pltpu.SMEM((16,), jnp.int32),
            vmem((VOCAB, CH), bf16),
            vmem((TAPS, CH, OWN), bf16),
            vmem((TAPS, CH, OWN), bf16),
            vmem((ROWS, CH), bf16),
            vmem((ROWS, CH), bf16),
            vmem((ROWS, CH), bf16),
            vmem((8, 128), f32),
            vmem((ZN, 128), f32),
            vmem((CH, CH), bf16),
            vmem((8, CH), f32),
            vmem((ROWS, OWN), f32),
            vmem((ROWS, CH), f32),
            vmem((MN, ROWS, OWN), bf16),
            vmem((ROWS, OWN), f32),
            vmem((MN, ROWS, OWN), f32),
            vmem((ROWS, 128), f32),
            vmem((ROWS, OWN), f32),
            vmem((MN, 8, 128), f32),
            vmem((CH, ROWS), bf16),
            vmem((CH, ROWS), bf16),
            vmem((SLICE, AN * ROWS), bf16),
            vmem((SLICE, AN * ROWS), bf16),
            vmem((ROWS, OWN), bf16),
            vmem((ROWS, OWN), bf16),
            vmem((AN, ZN + 2 * HALO1, RES, OWN), bf16),
            vmem((AN, ZN + 2 * HALO2, RES, OWN), bf16),
            vmem((2, 2, ROWS, OWN), bf16),
            vmem((MN, ROWS, OWN), bf16),
            vmem((2, ROWS, OWN), bf16),
            vmem((MN, ROWS, OWN), bf16),
            vmem((8, 128), f32),
            vmem((MN, 8, 128), f32),
            vmem((BN, PIECE1, OWN), bf16),
            vmem((BN, PIECE1, OWN), bf16),
            vmem((BN, PIECE2, OWN), bf16),
            vmem((BN, PIECE2, OWN), bf16),
            vmem((CH, CH), bf16),
            vmem((2, ROWS, OWN), bf16),
            vmem((2 * ZN, 2, RES, OWN), bf16),
            vmem((2, ROWS, OWN), bf16),
            pltpu.SemaphoreType.DMA((copies,)),
            pltpu.SemaphoreType.DMA((copies,)),
            pltpu.SemaphoreType.DMA((10,)),
            pltpu.SemaphoreType.REGULAR,
        ],
        compiler_params=pltpu.CompilerParams(
            collective_id=0, has_side_effects=True, vmem_limit_bytes=40 * 1024 * 1024
        ),
    )(*(pltpu.with_memory_space_constraint(v, pltpu.HBM) for v in operands))


def solution(mesh):
    placed = (P("seq", None), P("seq"), P("seq"), P(None, None, "mp"), P(None, None, "mp"), P())
    return jax.shard_map(
        local,
        mesh=mesh,
        in_specs=placed,
        out_specs=(P("seq", None), P(None, "seq", "mp"), P(None, "seq", "mp")),
        check_vma=False,
    )
```

```python
import functools
import itertools

import jax
import jax.numpy as jnp
from jax import lax
from jax.experimental import pallas as pl
from jax.experimental.pallas import tpu as pltpu
from jax.sharding import PartitionSpec as P

MESH = pl.DeviceIdType.MESH
ZN, XN, YN, MN = 8, 2, 8, 4
ROWS, CH, OWN, TAPS, VOCAB = 128, 512, 128, 9, 5
RES = ROWS // ZN
MID = TAPS // 2
HOP1, HOP2 = 1, 2
REACH1, REACH2 = 4, 3
HALO1, HALO2 = REACH1 * HOP1, REACH2 * HOP2
PIECE1, PIECE2 = 48, 32
AN, BN = 8, 16
SLICE = CH // AN

epsilon = 1e-05
root_half = 0.7071067811865476
inv_root_two_pi = 0.3989422804014327


def nn(a, b):
    return lax.dot_general(a, b, (((1,), (0,)), ((), ())), preferred_element_type=jnp.float32)


def nt(a, b):
    return lax.dot_general(a, b, (((1,), (1,)), ((), ())), preferred_element_type=jnp.float32)


def split_dot(left, values):
    high = values.astype(jnp.bfloat16)
    low = (values - high.astype(jnp.float32)).astype(jnp.bfloat16)
    return nt(left, high) + nt(left, low)


def gelu_parts(conv_out):
    normal_cdf = 0.5 * (1.0 + lax.erf(conv_out * root_half))
    slope = normal_cdf + conv_out * inv_root_two_pi * jnp.exp(-0.5 * conv_out * conv_out)
    return conv_out * normal_cdf, slope


class Group:
    def __init__(self, coords, mods, place):
        self.coords, self.mods, self.place = coords, mods, place
        every = itertools.product(*(range(n) for n in mods))
        distance = lambda off: sum(min(o, n - o) for o, n in zip(off, mods))
        self.offsets = sorted((o for o in every if any(o)), key=lambda o: -distance(o))

    def moved(self, off, back):
        return tuple(
            c if o == 0 else lax.rem(c + (n - o if back else o), n)
            for c, o, n in zip(self.coords, off, self.mods)
        )

    def index(self, coords):
        at = coords[0]
        for c, n in zip(coords[1:], self.mods[1:]):
            at = at * n + c
        return at

    def me(self):
        return self.index(self.coords)

    def to(self, off):
        coords = self.moved(off, False)
        return self.index(coords), self.place(coords)

    def source(self, off):
        return self.index(self.moved(off, True))


def conv(x_ref, k_ref, hop, reach, acc_ref):
    acc_ref[...] = nn(x_ref[...], k_ref[MID])
    for j in range(-reach, reach + 1):
        if j == 0:
            continue
        n = (ZN - abs(j) * hop) * RES
        to = max(0, -j * hop) * RES
        at = max(0, j * hop) * RES
        acc_ref[to : to + n, :] += nn(x_ref[at : at + n, :], k_ref[MID + j])


def back_conv(d_ref, k_ref, hop, reach, acc_ref):
    acc_ref[...] = nt(d_ref[...], k_ref[MID])
    for j in range(-reach, reach + 1):
        if j == 0:
            continue
        n = (ZN - abs(j) * hop) * RES
        to = max(0, j * hop) * RES
        at = max(0, -j * hop) * RES
        acc_ref[to : to + n, :] += nt(d_ref[at : at + n, :], k_ref[MID + j])


def back_conv_part(d_ref, k_ref, hop, reach, part, acc_ref):
    channels = pl.ds(pl.multiple_of(part * OWN, OWN), OWN)
    acc_ref[...] = nt(d_ref[...], k_ref[MID, channels, :])
    for j in range(-reach, reach + 1):
        if j == 0:
            continue
        n = (ZN - abs(j) * hop) * RES
        to = max(0, j * hop) * RES
        at = max(0, -j * hop) * RES
        acc_ref[to : to + n, :] += nt(d_ref[at : at + n, :], k_ref[MID + j, channels, :])


def tap_gradients(ht_ref, d_ref, hop, reach, halo):
    left = ht_ref[...]
    out = []
    for j in range(-reach, reach + 1):
        at = halo - j * hop
        right = d_ref[:, at : at + ZN, :, :].reshape(AN * ROWS, OWN)
        out.append(nn(left, right))
    return out


def pieces(grads, send_ref, first):
    half = lax.broadcasted_iota(jnp.int32, (8, OWN), 0) < 4
    for t in range(SLICE // 8):
        even, odd = [], []
        for a, b in zip(grads[::2], grads[1::2]):
            a, b = a[8 * t : 8 * t + 8], b[8 * t : 8 * t + 8]
            even.append(jnp.where(half, a, pltpu.roll(b, 4, 0)))
            odd.append(jnp.where(half, pltpu.roll(a, 4, 0), b))
        last = first + 8 * len(even)
        send_ref[2 * t, first:last] = jnp.concatenate(even, axis=0).astype(jnp.bfloat16)
        send_ref[2 * t + 1, first:last] = jnp.concatenate(odd, axis=0).astype(jnp.bfloat16)


def kernel(
    h_ref, ids_hbm, mask_hbm, k1_hbm, k2_hbm, w_hbm,
    out_ref, dk1_ref, dk2_ref,
    ids_ref, mask_ref, w_ref, k1, k2, hv, x0, x1, tsend, tgot, perm, w8, acc, wide,
    act1, slope1, norm1, inv1, slope2, stat,
    hsend0, hsend1, ht0, ht1, d1, d2, dpad1, dpad2,
    psend1, psend2, pgot1, pgot2, rsend, rgot,
    gsend, ggot, gsend2, ggot2, perm2, zsend, zgot, final,
    send_sems, recv_sems, local_sems, ready_x,
):
    f32, bf16 = jnp.float32, jnp.bfloat16
    s, m = lax.axis_index("seq"), lax.axis_index("mp")
    z = s // (XN * YN)
    xl = lax.rem(s // YN, XN)
    y = lax.rem(s, YN)
    seq_of = lambda z, x, y: (z * XN + x) * YN + y

    zs = Group((z,), (ZN,), lambda c: (seq_of(c[0], xl, y), m))
    core, xh = lax.rem(m, 2), m // 2
    ms = Group((xh, core), (2, 2), lambda c: (s, c[0] * 2 + c[1]))
    ys = Group((y,), (YN,), lambda c: (seq_of(z, xl, c[0]), m))
    xs = Group((xl,), (XN,), lambda c: (seq_of(z, c[0], y), m))
    cs = Group((core,), (2,), lambda c: (s, xh * 2 + c[0]))
    zx = Group((z, xh), (ZN, 2), lambda c: (seq_of(c[0], xl, y), c[1] * 2 + core))
    ga = ys
    gb = Group((z, xl), (ZN, XN), lambda c: (seq_of(c[0], c[1], y), m))
    gb2 = Group((xl, y), (XN, YN), lambda c: (seq_of(z, c[0], c[1]), m))
    seq_at = lambda a, b: seq_of(b >> 1, b & 1, a)

    count = itertools.count()
    started = []

    class Exchange:
        def __init__(self, group, bytes_of_all):
            self.group, self.i = group, next(count)
            self.all = self.copy(bytes_of_all, bytes_of_all, group.to(group.offsets[0])[1])

        def copy(self, src, dst, device):
            return pltpu.make_async_remote_copy(
                src_ref=src, dst_ref=dst, send_sem=send_sems.at[self.i], recv_sem=recv_sems.at[self.i],
                device_id=device, device_id_type=MESH,
            )

        def start(self, src_of, dst_of, chosen=lambda off: True):
            for off in filter(chosen, self.group.offsets):
                to, device = self.group.to(off)
                self.copy(src_of(to), dst_of(self.group.me()), device).start()
            if self not in started:
                started.append(self)

        def start_one(self, off, src, dst):
            self.copy(src, dst, self.group.to(off)[1]).start()
            if self not in started:
                started.append(self)

        def wait(self):
            self.all.wait_recv()

        def wait_send(self):
            self.all.wait_send()

    rows16 = lambda i: pl.ds(pl.multiple_of(i * RES, RES), RES)
    lanes = lambda i: pl.ds(pl.multiple_of(i * 128, 128), 128)
    slices = lambda i: pl.ds(pl.multiple_of(i * SLICE, SLICE), SLICE)

    barrier = pltpu.get_barrier_semaphore()
    seen = 0
    for group in (zs, ys, ms, xs):
        for off in group.offsets:
            pl.semaphore_signal(barrier, inc=1, device_id=group.to(off)[1], device_id_type=MESH)
            seen += 1

    load_h = pltpu.make_async_copy(h_ref, hv, local_sems.at[0])
    load_k1 = pltpu.make_async_copy(k1_hbm, k1, local_sems.at[1])
    load_k2 = pltpu.make_async_copy(k2_hbm, k2, local_sems.at[2])
    load_ids = pltpu.make_async_copy(ids_hbm, ids_ref, local_sems.at[4])
    load_mask = pltpu.make_async_copy(mask_hbm, mask_ref, local_sems.at[5])
    load_w = pltpu.make_async_copy(w_hbm, w_ref, local_sems.at[6])
    load_h.start()
    load_k1.start()
    load_ids.start()
    load_mask.start()
    load_w.start()
    load_k2.start()

    load_h.wait()
    pl.semaphore_wait(barrier, seen)

    move_h = Exchange(zs, x0.at[pl.ds(0, ROWS - RES)])
    move_h.start(lambda to: hv.at[rows16(to)], lambda me: x0.at[rows16(me)])
    x0[rows16(z), :] = hv[rows16(z), :]
    pl.semaphore_signal(ready_x, inc=1, device_id=xs.to((1,))[1], device_id_type=MESH)

    load_ids.wait()
    load_mask.wait()
    lane = lax.broadcasted_iota(jnp.int32, (8, 128), 1)
    sub = lax.broadcasted_iota(jnp.int32, (8, 128), 0)
    position = lane + s * ROWS
    hit = position == mask_ref[0]
    for q in range(1, 16):
        hit = jnp.logical_or(hit, position == mask_ref[q])
    target = jnp.where(hit, jnp.broadcast_to(ids_ref[...], (8, 128)), -1).astype(f32)
    target = pltpu.roll(target, z * RES, 1)
    tsend[...] = target
    row = lambda i: pl.ds(i, 1)
    move_t = Exchange(zs, tgot.at[pl.ds(0, ZN - 1)])
    move_t.start(lambda to: tsend.at[row(0)], lambda me: tgot.at[row(me)])
    tgot[row(z), :] = target[0:1]

    p = lax.broadcasted_iota(jnp.int32, (CH, 128), 0)
    a, b, low = p >> 6, (p >> 2) & (BN - 1), p & 3
    channel = seq_at(a, b) * 4 + low - lax.broadcasted_iota(jnp.int32, (CH, 128), 1)
    same = p - lax.broadcasted_iota(jnp.int32, (CH, 128), 1)
    for i in range(CH // 128):
        perm[:, i * 128 : i * 128 + 128] = (channel == i * 128).astype(f32).astype(bf16)
        perm2[:, i * 128 : i * 128 + 128] = (same == i * 128).astype(f32).astype(bf16)

    load_w.wait()
    w8[...] = jnp.concatenate([w_ref[...].astype(f32), jnp.zeros((8 - VOCAB, CH), f32)], axis=0)
    for dpad, halo in ((dpad1, HALO1), (dpad2, HALO2)):
        zero = jnp.zeros((AN, halo, RES, OWN), bf16)
        dpad[:, 0:halo] = zero
        dpad[:, halo + ZN : 2 * halo + ZN] = zero

    load_k1.wait()
    move_h.wait()

    conv(x0, k1, HOP1, REACH1, acc)
    activation, slope = gelu_parts(acc[...])
    slope1[...] = slope
    act1[m] = activation.astype(bf16)
    gather1 = Exchange(ms, act1.at[pl.ds(0, MN - 1)])
    gather1.start(lambda to: act1.at[m], lambda me: act1.at[me])

    mine = ga.me()
    hsend0[...] = nt(perm[...], x0[...]).astype(bf16)
    ht0[:, lanes(mine)] = hsend0[slices(mine), :]
    move0 = Exchange(ga, ht0.at[:, pl.ds(0, (AN - 1) * ROWS)])
    move0.start(lambda to: hsend0.at[slices(to)], lambda me: ht0.at[:, lanes(me)])
    move_t.wait()
    load_k2.wait()
    gather1.wait()

    values = jnp.concatenate([act1[i] for i in range(MN)], axis=1).astype(f32)
    centred = values - jnp.mean(values, axis=1, keepdims=True)
    inverse = lax.rsqrt(jnp.mean(centred * centred, axis=1, keepdims=True) + epsilon)
    normed = centred * inverse
    for i in range(MN):
        norm1[i] = normed[:, i * 128 : i * 128 + 128]
    inv1[...] = jnp.broadcast_to(inverse, (ROWS, 128))
    x1[...] = (x0[...].astype(f32) + normed).astype(bf16)

    conv(x1, k2, HOP2, REACH2, acc)
    activation, slope = gelu_parts(acc[...])
    slope2[...] = slope
    act2 = activation.astype(bf16)
    values2 = act2.astype(f32)
    w_own = w8[:, lanes(m)]
    sub_own = lax.broadcasted_iota(jnp.int32, (8, OWN), 0)
    left = jnp.where(sub_own == VOCAB, 1.0, w_own).astype(bf16)
    ones = jnp.ones((8, OWN), bf16)
    off_mean = values2 - jnp.mean(values2, axis=1, keepdims=True)
    sums = nt(left, act2)
    squares = split_dot(ones, off_mean * off_mean)
    stat[m] = jnp.where(sub == VOCAB + 1, squares, sums)
    share = Exchange(ms, stat.at[pl.ds(0, MN - 1)])
    share.start(lambda to: stat.at[m], lambda me: stat.at[me])

    hsend1[...] = nt(perm2[...], x1[...]).astype(bf16)
    ht1[:, lanes(z)] = hsend1[slices(z), :]
    move1 = Exchange(zs, ht1.at[:, pl.ds(0, (AN - 1) * ROWS)])
    move1.start(lambda to: hsend1.at[slices(to)], lambda me: ht1.at[:, lanes(me)])
    own_logits = nt(w8[...].astype(bf16), x1[...])
    w_sum = jnp.sum(w8[...], axis=1, keepdims=True)
    turned = pltpu.roll(tgot[...], lax.rem(ROWS - z * RES, ROWS), 1)
    targets = jnp.sum(jnp.where(lane // RES == sub, turned, 0.0), axis=0, keepdims=True)
    share.wait()

    each = [stat[i] for i in range(MN)]
    total = each[0] + each[1] + each[2] + each[3]
    mean2 = total[VOCAB : VOCAB + 1] * (1.0 / CH)
    spread = total[VOCAB + 1 : VOCAB + 2]
    for part in each:
        apart = part[VOCAB : VOCAB + 1] * (1.0 / OWN) - mean2
        spread = spread + OWN * apart * apart
    inv2 = lax.rsqrt(spread * (1.0 / CH) + epsilon)
    along = inv2 * (total - mean2 * w_sum)
    logits = own_logits + along
    classes = sub < VOCAB
    exponent = jnp.where(classes, jnp.exp(logits), 0.0)
    probability = exponent / jnp.sum(exponent, axis=0, keepdims=True)
    onehot = (sub.astype(f32) == targets).astype(f32)
    dlogits = jnp.where(jnp.logical_and(classes, targets >= 0.0), probability - onehot, 0.0)
    mean_grad = jnp.sum(dlogits * w_sum, axis=0, keepdims=True) * (1.0 / CH)
    mean_cross = jnp.sum(jnp.where(classes, dlogits * along, 0.0), axis=0, keepdims=True) * (1.0 / CH)
    slant = inv2 * mean_cross
    shift = mean_grad - slant * mean2
    packed = jnp.where(sub == 5, inv2, jnp.where(sub == 6, shift, jnp.where(sub == 7, slant, dlogits)))
    by_row = jnp.transpose(jnp.concatenate([packed, jnp.zeros((ROWS - 8, 128), f32)], axis=0))
    grad2 = by_row[:, 0:1] * w_own[0:1]
    for v in range(1, VOCAB):
        grad2 = grad2 + by_row[:, v : v + 1] * w_own[v : v + 1]
    dconv = by_row[:, 5:6] * (grad2 - by_row[:, 6:7] - values2 * by_row[:, 7:8]) * slope2[...]
    dconv = dconv.astype(bf16)
    d2[...] = dconv
    dpad2[z, HALO2 : HALO2 + ZN] = dconv.reshape(ZN, RES, OWN)

    share2 = Exchange(zs, dpad2.at[pl.ds(0, AN - 1), pl.ds(HALO2, ZN)])
    share2.start(lambda to: dpad2.at[z, pl.ds(HALO2, ZN)], lambda me: dpad2.at[me, pl.ds(HALO2, ZN)])

    first = grad2
    second = grad2 * norm1[m]
    reduce2 = Exchange(ms, pgot2.at[pl.ds(0, MN - 1)])
    for step in ms.offsets + [(0, 0)]:
        i = ms.to(step)[0]
        back_conv_part(d2, k2, HOP2, REACH2, i, acc)
        part = acc[...].astype(bf16)
        if any(step):
            psend2[i] = part
            reduce2.start_one(step, psend2.at[i], pgot2.at[m])
        else:
            pgot2[m] = part
        part = part.astype(f32)
        first = first + part
        second = second + part * norm1[i]
    rows_sum = jnp.where(sub == 0, split_dot(ones, first), split_dot(ones, second))
    rsend[...] = rows_sum
    rgot[m] = rows_sum
    reduce_rows = Exchange(ms, rgot.at[pl.ds(0, MN - 1)])
    reduce_rows.start(lambda to: rsend, lambda me: rgot.at[me])

    reduce2.wait()
    reduce_rows.wait()
    grad1 = grad2
    for i in range(MN):
        grad1 = grad1 + pgot2[i].astype(f32)
    rows_sum = (rgot[0] + rgot[1] + rgot[2] + rgot[3]) * (1.0 / CH)
    by_row = jnp.transpose(jnp.concatenate([rows_sum, jnp.zeros((ROWS - 8, 128), f32)], axis=0))
    dconv = inv1[...] * (grad1 - by_row[:, 0:1] - norm1[m] * by_row[:, 1:2]) * slope1[...]
    dconv = dconv.astype(bf16)
    d1[...] = dconv
    dpad1[mine, HALO1 : HALO1 + ZN] = dconv.reshape(ZN, RES, OWN)
    share1 = Exchange(ga, dpad1.at[pl.ds(0, AN - 1), pl.ds(HALO1, ZN)])
    share1.start(lambda to: dpad1.at[mine, pl.ds(HALO1, ZN)], lambda me: dpad1.at[me, pl.ds(HALO1, ZN)])

    back_conv(d1, k1, HOP1, REACH1, wide)
    for c in range(2):
        for i in range(2):
            at = (i * 2 + c) * 128
            psend1[c, i] = wide[:, at : at + 128].astype(bf16)
    reduce1 = Exchange(cs, pgot1)
    reduce1.start(lambda to: psend1.at[to], lambda me: pgot1)
    wide[:, lanes(m)] += grad1

    move1.wait()
    share2.wait()
    owner, owner2 = gb.me(), gb2.me()
    nothing = jnp.zeros((SLICE, OWN), f32)
    pieces(tap_gradients(ht1, dpad2, HOP2, REACH2, HALO2) + [nothing], gsend2, 0)
    ggot2[owner2] = gsend2[owner2]
    pl.semaphore_wait(ready_x, XN - 1)
    scatter2 = Exchange(gb2, ggot2.at[pl.ds(0, BN - 1)])
    scatter2.start(lambda to: gsend2.at[to], lambda me: ggot2.at[me])

    reduce1.wait()
    for i in range(2):
        zsend[i] = (wide[:, lanes(i * 2 + core)] + pgot1[i].astype(f32)).astype(bf16)
    zgot[zx.me()] = zsend[:, rows16(z), :]
    move_back = Exchange(zx, zgot.at[pl.ds(0, 2 * ZN - 1)])
    move_back.start(lambda to: zsend.at[:, rows16(to // 2)], lambda me: zgot.at[me])

    move0.wait()
    share1.wait()
    pieces(tap_gradients(ht0, dpad1, HOP1, REACH1, HALO1) + [nothing] * 3, gsend, 0)
    ggot[owner] = gsend[owner]
    scatter = Exchange(gb, ggot.at[pl.ds(0, BN - 1)])
    scatter.start(lambda to: gsend.at[to], lambda me: ggot.at[me])

    move_back.wait()
    gather_out = Exchange(cs, out_ref.at[:, pl.ds(0, 2 * OWN)])
    keep = []
    for i in range(2):
        for r in range(ZN):
            total = zgot[2 * r, i].astype(f32) + zgot[2 * r + 1, i].astype(f32)
            final[i, r * RES : r * RES + RES] = total.astype(bf16)
        place = out_ref.at[:, lanes(i * 2 + core)]
        keep.append(pltpu.make_async_copy(final.at[i], place, local_sems.at[3 + 6 * i]))
        keep[i].start()
        gather_out.start(lambda to: final.at[i], lambda me: place)

    dk2_ref[0] = jnp.zeros((4, OWN), f32)
    dk2_ref[TAPS - 1] = jnp.zeros((4, OWN), f32)
    scatter2.wait()
    grads = ggot2[0].astype(f32)
    for i in range(1, BN):
        grads = grads + ggot2[i].astype(f32)
    for j in range(2 * REACH2 + 1):
        dk2_ref[MID - REACH2 + j] = grads[4 * j : 4 * j + 4]
    scatter.wait()
    grads = ggot[0].astype(f32)
    for i in range(1, BN):
        grads = grads + ggot[i].astype(f32)
    for j in range(TAPS):
        dk1_ref[j] = grads[4 * j : 4 * j + 4]

    gather_out.wait()
    for copy in keep:
        copy.wait()
    for exchange in started:
        exchange.wait_send()


def local(h, ids, mask_index, k1, k2, w):
    f32, bf16 = jnp.float32, jnp.bfloat16
    vmem = pltpu.VMEM
    inside = pl.BlockSpec(memory_space=pltpu.VMEM)
    hbm = pl.BlockSpec(memory_space=pltpu.HBM)
    copies = 15
    operands = (h, ids.reshape(1, ROWS), mask_index, k1, k2, w.T)
    return pl.pallas_call(
        kernel,
        out_shape=(
            jax.ShapeDtypeStruct((ROWS, CH), bf16),
            jax.ShapeDtypeStruct((TAPS, 4, OWN), f32),
            jax.ShapeDtypeStruct((TAPS, 4, OWN), f32),
        ),
        in_specs=[hbm] * 6,
        out_specs=(hbm, inside, inside),
        scratch_shapes=[
            vmem((1, ROWS), jnp.int32),
            pltpu.SMEM((16,), jnp.int32),
            vmem((VOCAB, CH), bf16),
            vmem((TAPS, CH, OWN), bf16),
            vmem((TAPS, CH, OWN), bf16),
            vmem((ROWS, CH), bf16),
            vmem((ROWS, CH), bf16),
            vmem((ROWS, CH), bf16),
            vmem((8, 128), f32),
            vmem((ZN, 128), f32),
            vmem((CH, CH), bf16),
            vmem((8, CH), f32),
            vmem((ROWS, OWN), f32),
            vmem((ROWS, CH), f32),
            vmem((MN, ROWS, OWN), bf16),
            vmem((ROWS, OWN), f32),
            vmem((MN, ROWS, OWN), f32),
            vmem((ROWS, 128), f32),
            vmem((ROWS, OWN), f32),
            vmem((MN, 8, 128), f32),
            vmem((CH, ROWS), bf16),
            vmem((CH, ROWS), bf16),
            vmem((SLICE, AN * ROWS), bf16),
            vmem((SLICE, AN * ROWS), bf16),
            vmem((ROWS, OWN), bf16),
            vmem((ROWS, OWN), bf16),
            vmem((AN, ZN + 2 * HALO1, RES, OWN), bf16),
            vmem((AN, ZN + 2 * HALO2, RES, OWN), bf16),
            vmem((2, 2, ROWS, OWN), bf16),
            vmem((MN, ROWS, OWN), bf16),
            vmem((2, ROWS, OWN), bf16),
            vmem((MN, ROWS, OWN), bf16),
            vmem((8, 128), f32),
            vmem((MN, 8, 128), f32),
            vmem((BN, PIECE1, OWN), bf16),
            vmem((BN, PIECE1, OWN), bf16),
            vmem((BN, PIECE2, OWN), bf16),
            vmem((BN, PIECE2, OWN), bf16),
            vmem((CH, CH), bf16),
            vmem((2, ROWS, OWN), bf16),
            vmem((2 * ZN, 2, RES, OWN), bf16),
            vmem((2, ROWS, OWN), bf16),
            pltpu.SemaphoreType.DMA((copies,)),
            pltpu.SemaphoreType.DMA((copies,)),
            pltpu.SemaphoreType.DMA((10,)),
            pltpu.SemaphoreType.REGULAR,
        ],
        compiler_params=pltpu.CompilerParams(
            collective_id=0, has_side_effects=True, vmem_limit_bytes=40 * 1024 * 1024
        ),
    )(*(pltpu.with_memory_space_constraint(v, pltpu.HBM) for v in operands))


def solution(mesh):
    placed = (P("seq", None), P("seq"), P("seq"), P(None, None, "mp"), P(None, None, "mp"), P())
    return jax.shard_map(
        local,
        mesh=mesh,
        in_specs=placed,
        out_specs=(P("seq", None), P(None, "seq", "mp"), P(None, "seq", "mp")),
        check_vma=False,
    )
```
